32 devices in a mesh: gx: 16 (over z, y, core), gy: 2 (over x).
Axes of the slice: x: 2, y: 2, z: 4, core: 2. Of those that a mesh axis runs over, the one named last changes fastest.
Arguments:
- moisture: float32 [2048, 20, 128], P(('gx', 'gy')), may hold values from 0.05 to 1
- diffusivity: float32 [2048, 20, 128], P(('gx', 'gy')), may hold values from 0.1 to 4
- rain: float32 [2048, 128], P(('gx', 'gy')), may hold values from 0 to 2
- head: float32 [50, 256, 256], P(None, 'gx', 'gy'), may hold values from -4 to 4
- conductivity: float32 [50, 256, 256], P(None, 'gx', 'gy'), may hold values from 0.05 to 1
- tile_ids: int32 [2048], P(('gx', 'gy')), may hold values from 0 to 1, as said below
- offsets: int32 [2048], P(('gx', 'gy')), may hold values from 0 to 15
- patch_ids: int32 [2048], P(('gx', 'gy')), may hold values from 0 to 7
- counts: int32 [32], P(('gx', 'gy')), may hold values from 48 to 64, as said below
Outputs:
- head_out: float32 [50, 256, 256], P(None, 'gx', 'gy')
- moisture_out: float32 [2048, 20, 128], P(('gx', 'gy'))
- patch_sums: float32 [256, 128], P(('gx', 'gy'))
The draws below stay inside these ranges and needn't reach their ends.
Inputs may be any that keep to these rules, and one draw needn't show every extreme that they name: `tile_ids`: only the first counts[d] block slots of device d are used; the others' entries are arbitrary. Among the used blocks of one device at most 32 name the same tile, and in every gx row one tile is named by exactly 32 used blocks of every device of that row. `counts`: some device uses all 64 slots in every draw.
All inputs are finite; a program needn't handle non-finite values.
Results may differ from the reference program's by a relative error of at most 0.00016.
Values sent between devices are 32-bit elements; how exact they have to be, the bound alone decides.
A program may use at most 64 MiB of HBM per device.

```python
import math
import jax
import jax.numpy as jnp
from jax import lax

NZ = 50
LAYERS = 20
COLS = 128
CX = 16
LB = 64
PATCH_DEV = 8
SWEEPS = 6
NX = 256
NY = 256
BLOCKS = 2048
PATCHES = 256
N_GX = 16
N_GY = 2


def block_layout(key):
    device_count = N_GX * N_GY
    half = LB // 2
    base_key = jax.random.fold_in(key, 11)
    key_count, key_star, key_other, key_order, key_rows, key_patch = jax.random.split(base_key, 6)
    used_counts = jax.random.randint(key_count, (device_count,), (half + LB) // 2, LB + 1)
    used_counts = jnp.where(jnp.arange(device_count) == 0, LB, used_counts).astype(jnp.int32)
    star_row = jax.random.randint(key_star, (N_GX,), 0, N_GY)
    star_dev = jnp.repeat(star_row, N_GY)
    stride = jax.random.randint(key_other, (device_count, LB), 1, N_GY)
    position = jnp.arange(LB, dtype=jnp.int32)
    ordered = jnp.where(position[None, :] < half, star_dev[:, None], (star_dev[:, None] + stride) % N_GY)
    scores = jax.random.randint(key_order, (device_count, LB), 0, 2 ** 20) * LB + position[None, :]
    scores = jnp.where(position[None, :] < used_counts[:, None], scores, 2 ** 28 + position[None, :])
    shuffle = jnp.argsort(scores, axis=1)
    tiles = jnp.take_along_axis(ordered, shuffle, axis=1).reshape(-1).astype(jnp.int32)
    grid_rows = jax.random.randint(key_rows, (device_count * LB,), 0, CX).astype(jnp.int32)
    patches = jax.random.randint(key_patch, (device_count * LB,), 0, PATCH_DEV).astype(jnp.int32)
    return (tiles, grid_rows, patches, used_counts)


def draw_tile_ids(key, part):
    return block_layout(key)[0]


def draw_offsets(key, part):
    return block_layout(key)[1]


def draw_patch_ids(key, part):
    return block_layout(key)[2]


def draw_counts(key, part):
    return block_layout(key)[3]


def draw_head(key, part):
    return jax.random.truncated_normal(key, -4.0, 4.0, (NZ, NX, NY), jnp.float32)


def block_scale(key, shape, shards, smallest, high):
    level, own = 1.0, jax.random.fold_in(key, 6)
    for dim, blocks in shards:
        heights = jnp.exp(jax.random.uniform(jax.random.fold_in(own, dim), (blocks,), jnp.float32, smallest / len(shards), high / len(shards)))
        level = level * jnp.repeat(heights, shape[dim] // blocks).reshape([-1 if axis == dim else 1 for axis in range(len(shape))])
    return level


def setup_inputs(seed: int = 0) -> dict:
    seeds = jax.random.split(jax.random.key(seed), 10)
    return {
        "moisture": jnp.clip(jnp.exp(math.log(1.0) - 2.9957323 * jax.random.uniform(seeds[0], (BLOCKS, LAYERS, COLS), jnp.float32) ** block_scale(seeds[0], (BLOCKS, LAYERS, COLS), ((0, 32),), -0.2, 0.2)), 0.05, 1.0),
        "diffusivity": jnp.clip(jnp.exp(math.log(4.0) - 3.6888794 * jax.random.uniform(seeds[1], (BLOCKS, LAYERS, COLS), jnp.float32) ** block_scale(seeds[1], (BLOCKS, LAYERS, COLS), ((0, 32),), -0.2, 0.2)), 0.1, 4.0),
        "rain": jnp.clip(2.0 * jax.random.uniform(seeds[2], (BLOCKS, COLS), jnp.float32) ** block_scale(seeds[2], (BLOCKS, COLS), ((0, 32),), -0.2, 0.2), 0.0, 2.0),
        "head": draw_head(jax.random.fold_in(seeds[9], 71), 0),
        "conductivity": jnp.clip(jnp.exp(math.log(1.0) - 2.9957323 * jax.random.uniform(seeds[4], (NZ, NX, NY), jnp.float32) ** block_scale(seeds[4], (NZ, NX, NY), ((1, 16), (2, 2)), -0.2, 0.2)), 0.05, 1.0),
        "tile_ids": draw_tile_ids(jax.random.fold_in(seeds[9], 71), 0),
        "offsets": draw_offsets(jax.random.fold_in(seeds[9], 71), 0),
        "patch_ids": draw_patch_ids(jax.random.fold_in(seeds[9], 71), 0),
        "counts": draw_counts(jax.random.fold_in(seeds[9], 71), 0),
    }


flow_rate = 0.15
capillary = 0.5


def column_solve(moisture, diffusivity, rain):
    depth = moisture.shape[1]
    ratios = []
    forward_vals = []
    for layer_k in range(depth):
        lower_coef = diffusivity[:, layer_k, :]
        source = moisture[:, layer_k, :]
        if layer_k == 0:
            source = source + rain
            pivot = 1.0 + lower_coef
            carried = source / pivot
        else:
            upper_coef = diffusivity[:, layer_k - 1, :]
            pivot = 1.0 + lower_coef + upper_coef - upper_coef * ratios[-1]
            carried = (source + upper_coef * forward_vals[-1]) / pivot
        ratios.append(lower_coef / pivot)
        forward_vals.append(carried)
    solved = [forward_vals[-1]]
    for layer_k in range(depth - 2, -1, -1):
        solved.append(forward_vals[layer_k] + ratios[layer_k] * solved[-1])
    return jnp.stack(solved[::-1], axis=1)


def lateral_core(padded_head, padded_cond):
    inner_rows = padded_head.shape[1] - 2
    inner_cols = padded_head.shape[2] - 2
    centre = padded_head[:, 1:-1, 1:-1]
    centre_cond = padded_cond[:, 1:-1, 1:-1]
    flux_total = jnp.zeros_like(centre)
    for row_shift, col_shift in ((0, 1), (2, 1), (1, 0), (1, 2)):
        beside = padded_head[:, row_shift:row_shift + inner_rows, col_shift:col_shift + inner_cols]
        beside_cond = padded_cond[:, row_shift:row_shift + inner_rows, col_shift:col_shift + inner_cols]
        flux_total = flux_total + 0.5 * (centre_cond + beside_cond) * (beside - centre)
    vertical = 0.5 * (centre_cond[1:] + centre_cond[:-1]) * (centre[1:] - centre[:-1])
    flux_total = flux_total + jnp.pad(vertical, ((0, 1), (0, 0), (0, 0))) - jnp.pad(vertical, ((1, 0), (0, 0), (0, 0)))
    return centre + flow_rate * flux_total


def solve_group(grouped):
    return column_solve(grouped[0], grouped[1], grouped[2])


def reference(moisture, diffusivity, rain, head, conductivity, tile_ids, offsets, patch_ids, counts):
    device_count = N_GX * N_GY
    wet = lax.map(solve_group, (moisture.reshape(device_count, LB, LAYERS, COLS),
                                diffusivity.reshape(device_count, LB, LAYERS, COLS),
                                rain.reshape(device_count, LB, COLS)))
    wet = wet.reshape(BLOCKS, LAYERS, COLS)
    bottom = wet[:, LAYERS - 1, :]
    drain = diffusivity[:, LAYERS - 1, :] * bottom
    block_index = jnp.arange(BLOCKS, dtype=jnp.int32)
    owner = block_index // LB
    in_use = (block_index % LB) < counts[owner]
    in_use_f = in_use.astype(jnp.float32)
    grid_rows = (owner // N_GY) * CX + offsets
    grid_cols = tile_ids[:, None] * COLS + jnp.arange(COLS, dtype=jnp.int32)[None, :]
    surface = head[0].at[grid_rows[:, None], grid_cols].add(drain * in_use_f[:, None])
    field = head.at[0].set(surface)
    padding = ((0, 0), (1, 1), (1, 1))
    padded_cond = jnp.pad(conductivity, padding)
    for sweep_k in range(SWEEPS):
        field = lateral_core(jnp.pad(field, padding), padded_cond)
    saturation = field[0][grid_rows[:, None], grid_cols] * in_use_f[:, None]
    new_bottom = bottom + capillary * (saturation - in_use_f[:, None] * bottom)
    moisture_out = wet.at[:, LAYERS - 1, :].set(new_bottom)
    patch_global = owner * PATCH_DEV + patch_ids
    patch_sums = jax.ops.segment_sum(saturation, patch_global, num_segments=PATCHES)
    return (field, moisture_out, patch_sums)
```

```python
import functools

import jax
import jax.numpy as jnp
from jax import lax
from jax.experimental import pallas as pl
from jax.experimental.pallas import tpu as pltpu
from jax.sharding import PartitionSpec as P

PATCH_DEV = 8
SWEEPS = 6
HALO = 8
SLOT = 2 * HALO
LANES = 128
MESH = pl.DeviceIdType.MESH

flow_rate = 0.15
capillary = 0.5


def one_hot_rows(tile, offset, used_count, tile_count, tile_rows):
    blocks = tile.shape[1]
    block = lax.broadcasted_iota(jnp.int32, (1, blocks), 1)
    target = jnp.where(block < used_count, tile * tile_rows + offset, -1)
    slot = lax.broadcasted_iota(jnp.int32, (tile_count * tile_rows, blocks), 0)
    return (slot == target).astype(jnp.float32)


def flow_kernel(
    sizes,
    moist_in, diff_in, rain_in, head_in, cond_in, tile_ref, offset_ref, count_ref,
    field_out, wet_out, surf_out,
    h, k, w_e, w_s, w_v, delta, packed, land_l, land_r, moist, diff, ratio, rain,
    recharge, surf,
    local_sem, out_sem, row_send, row_recv, pack_send, pack_recv, rech_send, rech_recv,
    surf_send, surf_recv,
):
    rows_n, cols_n, nz, tile_rows = sizes
    gx, gy = lax.axis_index("gx"), lax.axis_index("gy")
    has_below, has_above = gx < rows_n - 1, gx > 0
    has_right, has_left = gy < cols_n - 1, gy > 0
    depth = moist.shape[0]
    groups = packed.shape[1]
    ring_rows, ring_cols = h.shape[1], h.shape[2]
    below = pl.ds(tile_rows, HALO)
    above = pl.ds(tile_rows + HALO, HALO)
    first = pl.ds(0, HALO)
    last = pl.ds(tile_rows - HALO, HALO)
    whole = pl.ds(0, tile_rows)
    main = pl.ds(0, LANES)

    local = [
        pltpu.make_async_copy(src, dst, local_sem.at[i])
        for i, (src, dst) in enumerate((
            (head_in, h.at[pl.ds(0, nz), whole, main]),
            (cond_in, k.at[pl.ds(0, nz), whole, main]),
            (moist_in, moist),
            (diff_in, diff),
            (rain_in, rain),
        ))
    ]
    for copy in local:
        copy.start()

    row_steps = ((0, None, whole, whole), (1, has_below, above, last), (-1, has_above, below, first))
    peers = []
    for dx, exists, _, _ in row_steps:
        for dy in range(cols_n):
            if dx or dy:
                peers.append((dx, exists, lax.rem(gy + dy, cols_n)))

    def when(cond, body):
        if cond is None:
            body()
        else:
            pl.when(cond)(body)

    def both(a, b):
        return b if a is None else jnp.logical_and(a, b)

    barrier = pltpu.get_barrier_semaphore()
    for dx, exists, col in peers:
        def greet(dx=dx, col=col):
            pl.semaphore_signal(barrier, inc=1, device_id=(gx + dx, col), device_id_type=MESH)
        when(exists, greet)
    near_rows = 1 + has_below.astype(jnp.int32) + has_above.astype(jnp.int32)
    pl.semaphore_wait(barrier, cols_n * near_rows - 1)

    row_copies = []
    for i, (dx, exists, ring, mine) in enumerate(row_steps[1:]):
        source_exists = has_above if dx == 1 else has_below
        for f, (src, dst) in enumerate(((head_in, h), (cond_in, k))):
            row_copies.append((exists, source_exists, pltpu.make_async_remote_copy(
                src_ref=src.at[:, mine],
                dst_ref=dst.at[pl.ds(0, nz), ring, main],
                send_sem=row_send.at[2 * i + f],
                recv_sem=row_recv.at[2 * i + f],
                device_id=(gx + dx, gy),
                device_id_type=MESH,
            )))
    for exists, _, copy in row_copies:
        when(exists, copy.start)

    local[0].wait()
    local[1].wait()
    lane = lax.broadcasted_iota(jnp.int32, (1, LANES), 1)

    def zero_tail(z, _):
        h[z] = jnp.zeros((ring_rows, ring_cols), jnp.float32)
        k[z] = jnp.zeros((ring_rows, ring_cols), jnp.float32)
        return 0
    lax.fori_loop(nz, h.shape[0], zero_tail, 0)

    def pack(g, _):
        for f, src in enumerate((h, k)):
            total = jnp.zeros((tile_rows, LANES), jnp.float32)
            for s in range(LANES // SLOT):
                edge = pltpu.roll(src[g * (LANES // SLOT) + s, 0:tile_rows, 0:LANES], (HALO + SLOT * s) % LANES, 1)
                inside = (lane >= SLOT * s) & (lane < SLOT * (s + 1))
                total = jnp.where(inside, edge, total)
            packed[f, g] = total
        return 0
    lax.fori_loop(0, groups, pack, 0)

    pack_copies = []
    n = 0
    for dx, exists, ring, mine in row_steps:
        source_row = None if dx == 0 else (has_above if dx == 1 else has_below)
        for dy, side, target, source in ((1, land_l, has_right, has_left), (-1, land_r, has_left, has_right)):
            pack_copies.append((both(exists, target), both(source_row, source), pltpu.make_async_remote_copy(
                src_ref=packed.at[:, :, mine],
                dst_ref=side.at[:, :, ring],
                send_sem=pack_send.at[n],
                recv_sem=pack_recv.at[n],
                device_id=(gx + dx, gy + dy),
                device_id_type=MESH,
            )))
            n += 1
    for exists, _, copy in pack_copies:
        when(exists, copy.start)

    for copy in local[2:]:
        copy.wait()
    e0 = diff[0]
    inv = 1.0 / (1.0 + e0)
    r0, f0 = e0 * inv, (moist[0] + rain[...]) * inv
    ratio[0] = r0
    moist[0] = f0

    def eliminate(layer, carry):
        upper, r, f = carry
        lower = diff[layer]
        inv = 1.0 / (1.0 + lower + upper - upper * r)
        r, f = lower * inv, (moist[layer] + upper * f) * inv
        ratio[layer] = r
        moist[layer] = f
        return lower, r, f
    lower, _, bottom = lax.fori_loop(1, depth, eliminate, (e0, r0, f0))
    drain = lower * bottom
    hot = one_hot_rows(tile_ref[...], offset_ref[...], count_ref[0], cols_n, tile_rows)
    mine = jnp.dot(hot, drain, precision=lax.Precision.HIGHEST, preferred_element_type=jnp.float32)
    recharge[0, gy] = mine.reshape(cols_n, tile_rows, LANES)

    rech_copies = []
    n = 0
    for i, (dx, exists, _, rows) in enumerate(row_steps):
        source_row = None if dx == 0 else (has_above if dx == 1 else has_below)
        for dy in range(0 if dx else 1, cols_n):
            to = lax.rem(gy + dy, cols_n)
            came = lax.rem(gy + cols_n - dy, cols_n)
            def copy(slot, to=to, dx=dx, i=i, rows=rows, n=n):
                return pltpu.make_async_remote_copy(
                    src_ref=recharge.at[0, gy, :, rows],
                    dst_ref=recharge.at[i, slot, :, rows],
                    send_sem=rech_send.at[n],
                    recv_sem=rech_recv.at[n],
                    device_id=(gx + dx, to),
                    device_id_type=MESH,
                )
            rech_copies.append((exists, source_row, copy(gy), copy(came)))
            n += 1
    for exists, _, out, _ in rech_copies:
        when(exists, out.start)

    def substitute(i, wet):
        layer = depth - 2 - i
        wet = moist[layer] + ratio[layer] * wet
        moist[layer] = wet
        return wet
    lax.fori_loop(0, depth - 1, substitute, bottom)
    wet_copy = pltpu.make_async_copy(moist, wet_out, out_sem.at[0])
    wet_copy.start()

    ring_row = lax.broadcasted_iota(jnp.int32, (ring_rows, ring_cols), 0)
    ring_col = lax.broadcasted_iota(jnp.int32, (ring_rows, ring_cols), 1)
    row_ok = (ring_row < tile_rows) | ((ring_row < tile_rows + HALO) & has_below) | ((ring_row >= tile_rows + HALO) & has_above)
    col_ok = (ring_col < LANES) | ((ring_col < LANES + LANES // 2) & has_right) | ((ring_col >= LANES + LANES // 2) & has_left)
    mask = (row_ok & col_ok).astype(jnp.float32)
    on_grid = mask > 0.0

    for _, source, copy in row_copies + pack_copies:
        when(source, copy.wait_recv)

    def unpack(g, _):
        for f, dst in enumerate((h, k)):
            comb = jnp.where((lane % SLOT) < HALO, land_l[f, g], land_r[f, g])
            for s in range(LANES // SLOT):
                z = g * (LANES // SLOT) + s
                side = pltpu.roll(comb, (LANES - HALO - SLOT * s) % LANES, 1)
                full = jnp.concatenate([dst[z, :, 0:LANES], side], axis=1)
                dst[z] = jnp.where(on_grid, full, 0.0)
        return 0
    lax.fori_loop(0, groups, unpack, 0)

    scale = 0.5 * flow_rate

    def weights(z, here):
        after = k[z + 1]
        w_e[z] = scale * (here + pltpu.roll(here, ring_cols - 1, 1))
        w_s[z] = scale * (here + pltpu.roll(here, ring_rows - 1, 0))
        w_v[z] = jnp.where(z < nz - 1, scale, 0.0) * (here + after)
        return after
    lax.fori_loop(0, nz, weights, k[0])

    def step(cells, z, carry, last):
        here, f_up = carry
        f_e = w_e[z] * (pltpu.roll(here, ring_cols - 1, 1) - here)
        f_s = w_s[z] * (pltpu.roll(here, ring_rows - 1, 0) - here)
        if last:
            after, f_v = here, jnp.zeros_like(here)
        else:
            after = cells[z + 1]
            f_v = w_v[z] * (after - here)
        change = (f_e - pltpu.roll(f_e, 1, 1)) + (f_s - pltpu.roll(f_s, 1, 0)) + (f_v - f_up)
        cells[z] = here + mask * change
        return after, f_v

    zeros = jnp.zeros((ring_rows, ring_cols), jnp.float32)

    def base_sweep(_, c):
        carry = lax.fori_loop(0, nz - 1, lambda z, carry: step(h, z, carry, False), (h[0], zeros))
        step(h, nz - 1, carry, True)
        return c
    lax.fori_loop(0, SWEEPS, base_sweep, 0)

    for _, source, _, arrived in rech_copies:
        when(source, arrived.wait_recv)

    def tile_sum(tile):
        parts = []
        for i, rows in ((0, whole), (1, last), (2, first)):
            total = recharge[i, 0, tile, rows]
            for s in range(1, cols_n):
                total = total + recharge[i, s, tile, rows]
            parts.append(total)
        return jnp.concatenate([parts[0], parts[2], parts[1]], axis=0)
    centre = tile_sum(gy)
    right = tile_sum(jnp.minimum(gy + 1, cols_n - 1))
    left = tile_sum(jnp.maximum(gy - 1, 0))
    side = jnp.where(lane < LANES // 2, right, left)
    delta[0] = jnp.where(on_grid, jnp.concatenate([centre, side], axis=1), 0.0)
    for z in range(1, SWEEPS + 2):
        delta[z] = zeros
    for sweep in range(SWEEPS):
        reach = min(sweep + 2, nz)
        lax.fori_loop(0, reach, lambda z, carry: step(delta, z, carry, False), (delta[0], zeros))
    for z in range(min(SWEEPS + 1, nz)):
        h[z, 0:tile_rows, 0:LANES] = h[z, 0:tile_rows, 0:LANES] + delta[z, 0:tile_rows, 0:LANES]

    surf[gy] = h[0, 0:tile_rows, 0:LANES]
    surf_copies = []
    for dy in range(1, cols_n):
        to = lax.rem(gy + dy, cols_n)
        came = lax.rem(gy + cols_n - dy, cols_n)
        pair = [
            pltpu.make_async_remote_copy(
                src_ref=surf.at[gy],
                dst_ref=surf.at[slot],
                send_sem=surf_send.at[dy - 1],
                recv_sem=surf_recv.at[dy - 1],
                device_id=(gx, to),
                device_id_type=MESH,
            )
            for slot in (gy, came)
        ]
        pair[0].start()
        surf_copies.append(pair)
    field_copy = pltpu.make_async_copy(h.at[pl.ds(0, nz), whole, main], field_out, out_sem.at[1])
    field_copy.start()
    for _, arrived in surf_copies:
        arrived.wait_recv()
    surf_copy = pltpu.make_async_copy(surf, surf_out, out_sem.at[2])
    surf_copy.start()

    for exists, _, copy in row_copies + pack_copies:
        when(exists, copy.wait_send)
    for exists, _, out, _ in rech_copies:
        when(exists, out.wait_send)
    for out, _ in surf_copies:
        out.wait_send()
    wet_copy.wait()
    field_copy.wait()
    surf_copy.wait()


def exchange_kernel(
    tile_rows, cols_n,
    field, wet, surf, tile_ref, offset_ref, patch_ref, count_ref,
    head_out, moist_out, patch_out,
    bottom, sem,
):
    depth, blocks, _ = wet.shape
    load = pltpu.make_async_copy(wet.at[depth - 1], bottom, sem.at[0])
    load.start()
    copies = [
        pltpu.make_async_copy(wet.at[pl.ds(0, depth - 1)], moist_out.at[pl.ds(0, depth - 1)], sem.at[1]),
        pltpu.make_async_copy(field, head_out, sem.at[2]),
    ]
    for copy in copies:
        copy.start()
    hot = one_hot_rows(tile_ref[...], offset_ref[...], count_ref[0], cols_n, tile_rows)
    surface = surf[...].reshape(cols_n * tile_rows, LANES)
    saturation = lax.dot_general(
        hot, surface, (((0,), (0,)), ((), ())),
        precision=lax.Precision.HIGHEST, preferred_element_type=jnp.float32,
    )
    patch = lax.broadcasted_iota(jnp.int32, (PATCH_DEV, blocks), 0)
    patch_hot = (patch == patch_ref[...]).astype(jnp.float32)
    patch_out[...] = jnp.dot(
        patch_hot, saturation, precision=lax.Precision.HIGHEST, preferred_element_type=jnp.float32
    )
    used = (lax.broadcasted_iota(jnp.int32, (blocks, LANES), 0) < count_ref[0]).astype(jnp.float32)
    load.wait()
    wet_bottom = bottom[...]
    bottom[...] = wet_bottom + capillary * (saturation - used * wet_bottom)
    store = pltpu.make_async_copy(bottom, moist_out.at[depth - 1], sem.at[0])
    store.start()
    store.wait()
    for copy in copies:
        copy.wait()


def local(rows_n, cols_n, moisture, diffusivity, rain, head, conductivity, tile_ids, offsets, patch_ids, counts):
    blocks, depth, _ = moisture.shape
    nz, tile_rows, _ = head.shape
    moisture = jnp.transpose(moisture, (1, 0, 2))
    diffusivity = jnp.transpose(diffusivity, (1, 0, 2))
    tile_ids, offsets, patch_ids = (x.reshape(1, blocks) for x in (tile_ids, offsets, patch_ids))
    f32 = jnp.float32
    per = LANES // SLOT
    groups = pl.cdiv(nz, per)
    ring = (tile_rows + 2 * HALO, 2 * LANES)
    hbm = pl.BlockSpec(memory_space=pl.ANY)
    vmem = pl.BlockSpec(memory_space=pltpu.VMEM)
    smem = pl.BlockSpec(memory_space=pltpu.SMEM)
    dma = pltpu.SemaphoreType.DMA
    rech = 3 * cols_n - 1
    field, wet, surf = pl.pallas_call(
        functools.partial(flow_kernel, (rows_n, cols_n, nz, tile_rows)),
        name="flow",
        out_shape=(
            jax.ShapeDtypeStruct((nz, tile_rows, LANES), f32),
            jax.ShapeDtypeStruct((depth, blocks, LANES), f32),
            jax.ShapeDtypeStruct((cols_n, tile_rows, LANES), f32),
        ),
        in_specs=[hbm] * 5 + [vmem] * 2 + [smem],
        out_specs=(hbm,) * 3,
        scratch_shapes=[
            pltpu.VMEM((groups * per,) + ring, f32),
            pltpu.VMEM((groups * per,) + ring, f32),
            pltpu.VMEM((nz,) + ring, f32),
            pltpu.VMEM((nz,) + ring, f32),
            pltpu.VMEM((nz,) + ring, f32),
            pltpu.VMEM((SWEEPS + 2,) + ring, f32),
            pltpu.VMEM((2, groups, tile_rows, LANES), f32),
            pltpu.VMEM((2, groups, ring[0], LANES), f32),
            pltpu.VMEM((2, groups, ring[0], LANES), f32),
            pltpu.VMEM((depth, blocks, LANES), f32),
            pltpu.VMEM((depth, blocks, LANES), f32),
            pltpu.VMEM((depth, blocks, LANES), f32),
            pltpu.VMEM((blocks, LANES), f32),
            pltpu.VMEM((3, cols_n, cols_n, tile_rows, LANES), f32),
            pltpu.VMEM((cols_n, tile_rows, LANES), f32),
            dma((5,)), dma((3,)), dma((4,)), dma((4,)), dma((6,)), dma((6,)),
            dma((rech,)), dma((rech,)), dma((cols_n,)), dma((cols_n,)),
        ],
        compiler_params=pltpu.CompilerParams(
            collective_id=0, has_side_effects=True, vmem_limit_bytes=32 * 1024 * 1024
        ),
    )(moisture, diffusivity, rain, head, conductivity, tile_ids, offsets, counts)
    head_out, moist_out, patch_sums = pl.pallas_call(
        functools.partial(exchange_kernel, tile_rows, cols_n),
        name="exchange",
        out_shape=(
            jax.ShapeDtypeStruct((nz, tile_rows, LANES), f32),
            jax.ShapeDtypeStruct((depth, blocks, LANES), f32),
            jax.ShapeDtypeStruct((PATCH_DEV, LANES), f32),
        ),
        in_specs=[hbm, hbm] + [vmem] * 4 + [smem],
        out_specs=(hbm, hbm, vmem),
        scratch_shapes=[pltpu.VMEM((blocks, LANES), f32), dma((3,))],
    )(field, wet, surf, tile_ids, offsets, patch_ids, counts)
    return head_out, jnp.transpose(moist_out, (1, 0, 2)), patch_sums


def solution(mesh):
    placed = (
        P(("gx", "gy"), None, None),
        P(("gx", "gy"), None, None),
        P(("gx", "gy"), None),
        P(None, "gx", "gy"),
        P(None, "gx", "gy"),
        P(("gx", "gy")),
        P(("gx", "gy")),
        P(("gx", "gy")),
        P(("gx", "gy")),
    )
    return jax.shard_map(
        functools.partial(local, mesh.shape["gx"], mesh.shape["gy"]),
        mesh=mesh,
        in_specs=placed,
        out_specs=(P(None, "gx", "gy"), P(("gx", "gy"), None, None), P(("gx", "gy"), None)),
        check_vma=False,
    )
```

```python
import functools

import jax
import jax.numpy as jnp
from jax import lax
from jax.experimental import pallas as pl
from jax.experimental.pallas import tpu as pltpu
from jax.sharding import PartitionSpec as P

PATCH_DEV = 8
SWEEPS = 6
HALO = 8
SLOT = 2 * HALO
LANES = 128
MESH = pl.DeviceIdType.MESH

flow_rate = 0.15
capillary = 0.5


def one_hot_rows(tile, offset, used_count, tile_count, tile_rows):
    blocks = tile.shape[1]
    block = lax.broadcasted_iota(jnp.int32, (1, blocks), 1)
    target = jnp.where(block < used_count, tile * tile_rows + offset, -1)
    slot = lax.broadcasted_iota(jnp.int32, (tile_count * tile_rows, blocks), 0)
    return (slot == target).astype(jnp.float32)


def flow_kernel(
    sizes,
    moist_in, diff_in, rain_in, head_in, cond_in, tile_in, offset_in, count_ref,
    field_out, wet_out, surf_out,
    h, k, w_e, w_s, w_v, delta, packed, land_l, land_r, moist, diff, ratio, rain,
    tile_ref, offset_ref, recharge, surf,
    local_sem, out_sem, row_send, row_recv, pack_send, pack_recv, rech_send, rech_recv,
    surf_send, surf_recv,
):
    rows_n, cols_n, nz, tile_rows = sizes
    gx, gy = lax.axis_index("gx"), lax.axis_index("gy")
    has_below, has_above = gx < rows_n - 1, gx > 0
    has_right, has_left = gy < cols_n - 1, gy > 0
    depth = moist.shape[0]
    groups = packed.shape[1]
    ring_rows, ring_cols = h.shape[1], h.shape[2]
    below = pl.ds(tile_rows, HALO)
    above = pl.ds(tile_rows + HALO, HALO)
    first = pl.ds(0, HALO)
    last = pl.ds(tile_rows - HALO, HALO)
    whole = pl.ds(0, tile_rows)
    main = pl.ds(0, LANES)

    local = [
        pltpu.make_async_copy(src, dst, local_sem.at[i])
        for i, (src, dst) in enumerate((
            (head_in, h.at[pl.ds(0, nz), whole, main]),
            (cond_in, k.at[pl.ds(0, nz), whole, main]),
            (moist_in, moist),
            (diff_in, diff),
            (rain_in, rain),
            (tile_in, tile_ref),
            (offset_in, offset_ref),
        ))
    ]
    for copy in local:
        copy.start()

    row_steps = ((0, None, whole, whole), (1, has_below, above, last), (-1, has_above, below, first))
    peers = []
    for dx, exists, _, _ in row_steps:
        for dy in range(cols_n):
            if dx or dy:
                peers.append((dx, exists, lax.rem(gy + dy, cols_n)))

    def when(cond, body):
        if cond is None:
            body()
        else:
            pl.when(cond)(body)

    def both(a, b):
        return b if a is None else jnp.logical_and(a, b)

    barrier = pltpu.get_barrier_semaphore()
    for dx, exists, col in peers:
        def greet(dx=dx, col=col):
            pl.semaphore_signal(barrier, inc=1, device_id=(gx + dx, col), device_id_type=MESH)
        when(exists, greet)
    near_rows = 1 + has_below.astype(jnp.int32) + has_above.astype(jnp.int32)
    pl.semaphore_wait(barrier, cols_n * near_rows - 1)

    row_copies = []
    for i, (dx, exists, ring, mine) in enumerate(row_steps[1:]):
        source_exists = has_above if dx == 1 else has_below
        for f, (src, dst) in enumerate(((head_in, h), (cond_in, k))):
            row_copies.append((exists, source_exists, pltpu.make_async_remote_copy(
                src_ref=src.at[:, mine],
                dst_ref=dst.at[pl.ds(0, nz), ring, main],
                send_sem=row_send.at[2 * i + f],
                recv_sem=row_recv.at[2 * i + f],
                device_id=(gx + dx, gy),
                device_id_type=MESH,
            )))
    for exists, _, copy in row_copies:
        when(exists, copy.start)

    local[0].wait()
    local[1].wait()
    lane = lax.broadcasted_iota(jnp.int32, (1, LANES), 1)

    def zero_tail(z, _):
        h[z] = jnp.zeros((ring_rows, ring_cols), jnp.float32)
        k[z] = jnp.zeros((ring_rows, ring_cols), jnp.float32)
        return 0
    lax.fori_loop(nz, h.shape[0], zero_tail, 0)

    def pack(g, _):
        for f, src in enumerate((h, k)):
            total = jnp.zeros((tile_rows, LANES), jnp.float32)
            for s in range(LANES // SLOT):
                edge = pltpu.roll(src[g * (LANES // SLOT) + s, 0:tile_rows, 0:LANES], (HALO + SLOT * s) % LANES, 1)
                inside = (lane >= SLOT * s) & (lane < SLOT * (s + 1))
                total = jnp.where(inside, edge, total)
            packed[f, g] = total
        return 0
    lax.fori_loop(0, groups, pack, 0)

    pack_copies = []
    n = 0
    for dx, exists, ring, mine in row_steps:
        source_row = None if dx == 0 else (has_above if dx == 1 else has_below)
        for dy, side, target, source in ((1, land_l, has_right, has_left), (-1, land_r, has_left, has_right)):
            pack_copies.append((both(exists, target), both(source_row, source), pltpu.make_async_remote_copy(
                src_ref=packed.at[:, :, mine],
                dst_ref=side.at[:, :, ring],
                send_sem=pack_send.at[n],
                recv_sem=pack_recv.at[n],
                device_id=(gx + dx, gy + dy),
                device_id_type=MESH,
            )))
            n += 1
    for exists, _, copy in pack_copies:
        when(exists, copy.start)

    for copy in local[2:]:
        copy.wait()
    e0 = diff[0]
    inv = 1.0 / (1.0 + e0)
    r0, f0 = e0 * inv, (moist[0] + rain[...]) * inv
    ratio[0] = r0
    moist[0] = f0

    def eliminate(layer, carry):
        upper, r, f = carry
        lower = diff[layer]
        inv = 1.0 / (1.0 + lower + upper - upper * r)
        r, f = lower * inv, (moist[layer] + upper * f) * inv
        ratio[layer] = r
        moist[layer] = f
        return lower, r, f
    lower, _, bottom = lax.fori_loop(1, depth, eliminate, (e0, r0, f0))
    drain = lower * bottom
    hot = one_hot_rows(tile_ref[...], offset_ref[...], count_ref[0], cols_n, tile_rows)
    mine = jnp.dot(hot, drain, precision=lax.Precision.HIGHEST, preferred_element_type=jnp.float32)
    recharge[0, gy] = mine.reshape(cols_n, tile_rows, LANES)

    rech_copies = []
    n = 0
    for i, (dx, exists, _, rows) in enumerate(row_steps):
        source_row = None if dx == 0 else (has_above if dx == 1 else has_below)
        for dy in range(0 if dx else 1, cols_n):
            to = lax.rem(gy + dy, cols_n)
            came = lax.rem(gy + cols_n - dy, cols_n)
            def copy(slot, to=to, dx=dx, i=i, rows=rows, n=n):
                return pltpu.make_async_remote_copy(
                    src_ref=recharge.at[0, gy, :, rows],
                    dst_ref=recharge.at[i, slot, :, rows],
                    send_sem=rech_send.at[n],
                    recv_sem=rech_recv.at[n],
                    device_id=(gx + dx, to),
                    device_id_type=MESH,
                )
            rech_copies.append((exists, source_row, copy(gy), copy(came)))
            n += 1
    for exists, _, out, _ in rech_copies:
        when(exists, out.start)

    def substitute(i, wet):
        layer = depth - 2 - i
        wet = moist[layer] + ratio[layer] * wet
        moist[layer] = wet
        return wet
    lax.fori_loop(0, depth - 1, substitute, bottom)
    wet_copy = pltpu.make_async_copy(moist, wet_out, out_sem.at[0])
    wet_copy.start()

    ring_row = lax.broadcasted_iota(jnp.int32, (ring_rows, ring_cols), 0)
    ring_col = lax.broadcasted_iota(jnp.int32, (ring_rows, ring_cols), 1)
    row_ok = (ring_row < tile_rows) | ((ring_row < tile_rows + HALO) & has_below) | ((ring_row >= tile_rows + HALO) & has_above)
    col_ok = (ring_col < LANES) | ((ring_col < LANES + LANES // 2) & has_right) | ((ring_col >= LANES + LANES // 2) & has_left)
    mask = (row_ok & col_ok).astype(jnp.float32)
    on_grid = mask > 0.0

    for _, source, copy in row_copies + pack_copies:
        when(source, copy.wait_recv)

    def unpack(g, _):
        for f, dst in enumerate((h, k)):
            comb = jnp.where((lane % SLOT) < HALO, land_l[f, g], land_r[f, g])
            for s in range(LANES // SLOT):
                z = g * (LANES // SLOT) + s
                side = pltpu.roll(comb, (LANES - HALO - SLOT * s) % LANES, 1)
                full = jnp.concatenate([dst[z, :, 0:LANES], side], axis=1)
                dst[z] = jnp.where(on_grid, full, 0.0)
        return 0
    lax.fori_loop(0, groups, unpack, 0)

    scale = 0.5 * flow_rate

    def weights(z, here):
        after = k[z + 1]
        w_e[z] = scale * (here + pltpu.roll(here, ring_cols - 1, 1))
        w_s[z] = scale * (here + pltpu.roll(here, ring_rows - 1, 0))
        w_v[z] = jnp.where(z < nz - 1, scale, 0.0) * (here + after)
        return after
    lax.fori_loop(0, nz, weights, k[0])

    def step(cells, z, carry, last):
        here, f_up = carry
        f_e = w_e[z] * (pltpu.roll(here, ring_cols - 1, 1) - here)
        f_s = w_s[z] * (pltpu.roll(here, ring_rows - 1, 0) - here)
        if last:
            after, f_v = here, jnp.zeros_like(here)
        else:
            after = cells[z + 1]
            f_v = w_v[z] * (after - here)
        change = (f_e - pltpu.roll(f_e, 1, 1)) + (f_s - pltpu.roll(f_s, 1, 0)) + (f_v - f_up)
        cells[z] = here + mask * change
        return after, f_v

    zeros = jnp.zeros((ring_rows, ring_cols), jnp.float32)

    def base_sweep(_, c):
        carry = lax.fori_loop(0, nz - 1, lambda z, carry: step(h, z, carry, False), (h[0], zeros))
        step(h, nz - 1, carry, True)
        return c
    lax.fori_loop(0, SWEEPS, base_sweep, 0)

    for _, source, _, arrived in rech_copies:
        when(source, arrived.wait_recv)

    def tile_sum(tile):
        parts = []
        for i, rows in ((0, whole), (1, last), (2, first)):
            total = recharge[i, 0, tile, rows]
            for s in range(1, cols_n):
                total = total + recharge[i, s, tile, rows]
            parts.append(total)
        return jnp.concatenate([parts[0], parts[2], parts[1]], axis=0)
    centre = tile_sum(gy)
    right = tile_sum(jnp.minimum(gy + 1, cols_n - 1))
    left = tile_sum(jnp.maximum(gy - 1, 0))
    side = jnp.where(lane < LANES // 2, right, left)
    delta[0] = jnp.where(on_grid, jnp.concatenate([centre, side], axis=1), 0.0)
    for z in range(1, SWEEPS + 2):
        delta[z] = zeros
    for sweep in range(SWEEPS):
        reach = min(sweep + 2, nz)
        lax.fori_loop(0, reach, lambda z, carry: step(delta, z, carry, False), (delta[0], zeros))
    for z in range(min(SWEEPS + 1, nz)):
        h[z, 0:tile_rows, 0:LANES] = h[z, 0:tile_rows, 0:LANES] + delta[z, 0:tile_rows, 0:LANES]

    surf[gy] = h[0, 0:tile_rows, 0:LANES]
    surf_copies = []
    for dy in range(1, cols_n):
        to = lax.rem(gy + dy, cols_n)
        came = lax.rem(gy + cols_n - dy, cols_n)
        pair = [
            pltpu.make_async_remote_copy(
                src_ref=surf.at[gy],
                dst_ref=surf.at[slot],
                send_sem=surf_send.at[dy - 1],
                recv_sem=surf_recv.at[dy - 1],
                device_id=(gx, to),
                device_id_type=MESH,
            )
            for slot in (gy, came)
        ]
        pair[0].start()
        surf_copies.append(pair)
    field_copy = pltpu.make_async_copy(h.at[pl.ds(0, nz), whole, main], field_out, out_sem.at[1])
    field_copy.start()
    for _, arrived in surf_copies:
        arrived.wait_recv()
    surf_copy = pltpu.make_async_copy(surf, surf_out, out_sem.at[2])
    surf_copy.start()

    for exists, _, copy in row_copies + pack_copies:
        when(exists, copy.wait_send)
    for exists, _, out, _ in rech_copies:
        when(exists, out.wait_send)
    for out, _ in surf_copies:
        out.wait_send()
    wet_copy.wait()
    field_copy.wait()
    surf_copy.wait()


def exchange_kernel(
    tile_rows, cols_n,
    field_in, wet_in, surf_in, tile_in, offset_in, patch_in, count_ref,
    head_out, moist_out, patch_out,
    field, wet, surf, tile_ref, offset_ref, patch_ref, sem,
):
    depth, blocks, _ = wet.shape
    upper = pl.ds(0, depth - 1)
    loads = [
        pltpu.make_async_copy(src, dst, sem.at[i])
        for i, (src, dst) in enumerate((
            (tile_in, tile_ref),
            (offset_in, offset_ref),
            (patch_in, patch_ref),
            (surf_in, surf),
            (wet_in.at[depth - 1], wet.at[depth - 1]),
            (wet_in.at[upper], wet.at[upper]),
            (field_in, field),
        ))
    ]
    for copy in loads:
        copy.start()
    for copy in loads[:5]:
        copy.wait()
    hot = one_hot_rows(tile_ref[...], offset_ref[...], count_ref[0], cols_n, tile_rows)
    surface = surf[...].reshape(cols_n * tile_rows, LANES)
    saturation = lax.dot_general(
        hot, surface, (((0,), (0,)), ((), ())),
        precision=lax.Precision.HIGHEST, preferred_element_type=jnp.float32,
    )
    patch = lax.broadcasted_iota(jnp.int32, (PATCH_DEV, blocks), 0)
    patch_hot = (patch == patch_ref[...]).astype(jnp.float32)
    patch_out[...] = jnp.dot(
        patch_hot, saturation, precision=lax.Precision.HIGHEST, preferred_element_type=jnp.float32
    )
    used = (lax.broadcasted_iota(jnp.int32, (blocks, LANES), 0) < count_ref[0]).astype(jnp.float32)
    wet_bottom = wet[depth - 1]
    wet[depth - 1] = wet_bottom + capillary * (saturation - used * wet_bottom)
    stores = [
        pltpu.make_async_copy(wet.at[depth - 1], moist_out.at[depth - 1], sem.at[0]),
        pltpu.make_async_copy(wet.at[upper], moist_out.at[upper], sem.at[1]),
        pltpu.make_async_copy(field, head_out, sem.at[2]),
    ]
    stores[0].start()
    for load, store in zip(loads[5:], stores[1:]):
        load.wait()
        store.start()
    for store in stores:
        store.wait()


def local(rows_n, cols_n, moisture, diffusivity, rain, head, conductivity, tile_ids, offsets, patch_ids, counts):
    blocks, depth, _ = moisture.shape
    nz, tile_rows, _ = head.shape
    moisture = jnp.transpose(moisture, (1, 0, 2))
    diffusivity = jnp.transpose(diffusivity, (1, 0, 2))
    tile_ids, offsets, patch_ids = (x.reshape(1, blocks) for x in (tile_ids, offsets, patch_ids))
    f32 = jnp.float32
    per = LANES // SLOT
    groups = pl.cdiv(nz, per)
    ring = (tile_rows + 2 * HALO, 2 * LANES)
    hbm = pl.BlockSpec(memory_space=pltpu.HBM)
    vmem = pl.BlockSpec(memory_space=pltpu.VMEM)
    smem = pl.BlockSpec(memory_space=pltpu.SMEM)
    dma = pltpu.SemaphoreType.DMA
    rech = 3 * cols_n - 1
    field, wet, surf = pl.pallas_call(
        functools.partial(flow_kernel, (rows_n, cols_n, nz, tile_rows)),
        name="flow",
        out_shape=(
            jax.ShapeDtypeStruct((nz, tile_rows, LANES), f32),
            jax.ShapeDtypeStruct((depth, blocks, LANES), f32),
            jax.ShapeDtypeStruct((cols_n, tile_rows, LANES), f32),
        ),
        in_specs=[hbm] * 7 + [smem],
        out_specs=(hbm,) * 3,
        scratch_shapes=[
            pltpu.VMEM((groups * per,) + ring, f32),
            pltpu.VMEM((groups * per,) + ring, f32),
            pltpu.VMEM((nz,) + ring, f32),
            pltpu.VMEM((nz,) + ring, f32),
            pltpu.VMEM((nz,) + ring, f32),
            pltpu.VMEM((SWEEPS + 2,) + ring, f32),
            pltpu.VMEM((2, groups, tile_rows, LANES), f32),
            pltpu.VMEM((2, groups, ring[0], LANES), f32),
            pltpu.VMEM((2, groups, ring[0], LANES), f32),
            pltpu.VMEM((depth, blocks, LANES), f32),
            pltpu.VMEM((depth, blocks, LANES), f32),
            pltpu.VMEM((depth, blocks, LANES), f32),
            pltpu.VMEM((blocks, LANES), f32),
            pltpu.VMEM((1, blocks), jnp.int32),
            pltpu.VMEM((1, blocks), jnp.int32),
            pltpu.VMEM((3, cols_n, cols_n, tile_rows, LANES), f32),
            pltpu.VMEM((cols_n, tile_rows, LANES), f32),
            dma((7,)), dma((3,)), dma((4,)), dma((4,)), dma((6,)), dma((6,)),
            dma((rech,)), dma((rech,)), dma((cols_n,)), dma((cols_n,)),
        ],
        compiler_params=pltpu.CompilerParams(
            collective_id=0, has_side_effects=True, vmem_limit_bytes=63 * 1024 * 1024
        ),
    )(moisture, diffusivity, rain, head, conductivity, tile_ids, offsets, counts)
    head_out, moist_out, patch_sums = pl.pallas_call(
        functools.partial(exchange_kernel, tile_rows, cols_n),
        name="exchange",
        out_shape=(
            jax.ShapeDtypeStruct((nz, tile_rows, LANES), f32),
            jax.ShapeDtypeStruct((depth, blocks, LANES), f32),
            jax.ShapeDtypeStruct((PATCH_DEV, LANES), f32),
        ),
        in_specs=[hbm] * 6 + [smem],
        out_specs=(hbm, hbm, vmem),
        scratch_shapes=[
            pltpu.VMEM((nz, tile_rows, LANES), f32),
            pltpu.VMEM((depth, blocks, LANES), f32),
            pltpu.VMEM((cols_n, tile_rows, LANES), f32),
            pltpu.VMEM((1, blocks), jnp.int32),
            pltpu.VMEM((1, blocks), jnp.int32),
            pltpu.VMEM((1, blocks), jnp.int32),
            dma((7,)),
        ],
        compiler_params=pltpu.CompilerParams(vmem_limit_bytes=63 * 1024 * 1024),
    )(field, wet, surf, tile_ids, offsets, patch_ids, counts)
    return head_out, jnp.transpose(moist_out, (1, 0, 2)), patch_sums


def solution(mesh):
    placed = (
        P(("gx", "gy"), None, None),
        P(("gx", "gy"), None, None),
        P(("gx", "gy"), None),
        P(None, "gx", "gy"),
        P(None, "gx", "gy"),
        P(("gx", "gy")),
        P(("gx", "gy")),
        P(("gx", "gy")),
        P(("gx", "gy")),
    )
    return jax.shard_map(
        functools.partial(local, mesh.shape["gx"], mesh.shape["gy"]),
        mesh=mesh,
        in_specs=placed,
        out_specs=(P(None, "gx", "gy"), P(("gx", "gy"), None, None), P(("gx", "gy"), None)),
        check_vma=False,
    )
```

```python
import functools

import jax
import jax.numpy as jnp
from jax import lax
from jax.experimental import pallas as pl
from jax.experimental.pallas import tpu as pltpu
from jax.sharding import PartitionSpec as P

PATCH_DEV = 8
SWEEPS = 6
HALO = 8
BLOCK = 5
SLOT = 2 * HALO
LANES = 128
MESH = pl.DeviceIdType.MESH

flow_rate = 0.15
capillary = 0.5


def one_hot_rows(tile, offset, used_count, tile_count, tile_rows):
    blocks = tile.shape[1]
    block = lax.broadcasted_iota(jnp.int32, (1, blocks), 1)
    target = jnp.where(block < used_count, tile * tile_rows + offset, -1)
    slot = lax.broadcasted_iota(jnp.int32, (tile_count * tile_rows, blocks), 0)
    return (slot == target).astype(jnp.float32)


def flow_kernel(
    sizes,
    moist_in, diff_in, rain_in, head_in, cond_in, tile_in, offset_in, count_ref,
    field_out, wet_out, surf_out,
    h, h2, k, field, w_d, w_e, w_w, w_s, w_n, w_v, delta, delta2, packed, land_l, land_r, moist, diff, ratio, rain,
    tile_ref, offset_ref, recharge, surf,
    local_sem, out_sem, row_send, row_recv, pack_send, pack_recv, rech_send, rech_recv,
    surf_send, surf_recv,
):
    rows_n, cols_n, nz, tile_rows = sizes
    gx, gy = lax.axis_index("gx"), lax.axis_index("gy")
    has_below, has_above = gx < rows_n - 1, gx > 0
    has_right, has_left = gy < cols_n - 1, gy > 0
    depth = moist.shape[0]
    groups = packed.shape[1]
    ring_rows, ring_cols = h.shape[1], h.shape[2]
    below = pl.ds(tile_rows, HALO)
    above = pl.ds(tile_rows + HALO, HALO)
    first = pl.ds(0, HALO)
    last = pl.ds(tile_rows - HALO, HALO)
    whole = pl.ds(0, tile_rows)
    main = pl.ds(0, LANES)
    layers = pl.ds(1, nz)

    local = [
        pltpu.make_async_copy(src, dst, local_sem.at[i])
        for i, (src, dst) in enumerate((
            (head_in, h.at[layers, whole, main]),
            (cond_in, k.at[layers, whole, main]),
            (moist_in, moist),
            (diff_in, diff),
            (rain_in, rain),
            (tile_in, tile_ref),
            (offset_in, offset_ref),
        ))
    ]
    for copy in local:
        copy.start()

    row_steps = ((0, None, whole, whole), (1, has_below, above, last), (-1, has_above, below, first))
    peers = []
    for dx, exists, _, _ in row_steps:
        for dy in range(cols_n):
            if dx or dy:
                peers.append((dx, exists, lax.rem(gy + dy, cols_n)))

    def when(cond, body):
        if cond is None:
            body()
        else:
            pl.when(cond)(body)

    def both(a, b):
        return b if a is None else jnp.logical_and(a, b)

    empty = jnp.zeros((ring_rows, ring_cols), jnp.float32)
    for ref in (h, h2, k):
        ref[0] = empty
        ref[nz + 1] = empty

    def clear(rows):
        def body(z, _):
            for ref in (h, k):
                ref[z, rows, main] = jnp.zeros((HALO, LANES), jnp.float32)
            return 0
        lax.fori_loop(1, nz + 1, body, 0)
    pl.when(gx == 0)(lambda: clear(above))
    pl.when(gx == rows_n - 1)(lambda: clear(below))

    barrier = pltpu.get_barrier_semaphore()
    for dx, exists, col in peers:
        def greet(dx=dx, col=col):
            pl.semaphore_signal(barrier, inc=1, device_id=(gx + dx, col), device_id_type=MESH)
        when(exists, greet)
    near_rows = 1 + has_below.astype(jnp.int32) + has_above.astype(jnp.int32)
    pl.semaphore_wait(barrier, cols_n * near_rows - 1)

    row_copies = []
    for i, (dx, exists, ring, mine) in enumerate(row_steps[1:]):
        source_exists = has_above if dx == 1 else has_below
        for f, (src, dst) in enumerate(((head_in, h), (cond_in, k))):
            row_copies.append((exists, source_exists, pltpu.make_async_remote_copy(
                src_ref=src.at[:, mine],
                dst_ref=dst.at[layers, ring, main],
                send_sem=row_send.at[2 * i + f],
                recv_sem=row_recv.at[2 * i + f],
                device_id=(gx + dx, gy),
                device_id_type=MESH,
            )))
    for exists, _, copy in row_copies:
        when(exists, copy.start)

    local[0].wait()
    local[1].wait()
    lane = lax.broadcasted_iota(jnp.int32, (1, LANES), 1)

    per = LANES // SLOT
    for g in range(groups):
        for f, src in enumerate((h, k)):
            total = jnp.zeros((tile_rows, LANES), jnp.float32)
            for s in range(min(per, nz - g * per)):
                edge = pltpu.roll(src[1 + g * per + s, 0:tile_rows, 0:LANES], (HALO + SLOT * s) % LANES, 1)
                inside = (lane >= SLOT * s) & (lane < SLOT * (s + 1))
                total = jnp.where(inside, edge, total)
            packed[f, g] = total

    pack_copies = []
    n = 0
    for dx, exists, ring, mine in row_steps:
        source_row = None if dx == 0 else (has_above if dx == 1 else has_below)
        for dy, side, target, source in ((1, land_l, has_right, has_left), (-1, land_r, has_left, has_right)):
            pack_copies.append((both(exists, target), both(source_row, source), pltpu.make_async_remote_copy(
                src_ref=packed.at[:, :, mine],
                dst_ref=side.at[:, :, ring],
                send_sem=pack_send.at[n],
                recv_sem=pack_recv.at[n],
                device_id=(gx + dx, gy + dy),
                device_id_type=MESH,
            )))
            n += 1
    for exists, _, copy in pack_copies:
        when(exists, copy.start)

    for copy in local[2:]:
        copy.wait()
    e0 = diff[0]
    inv = 1.0 / (1.0 + e0)
    r0, f0 = e0 * inv, (moist[0] + rain[...]) * inv
    ratio[0] = r0
    moist[0] = f0

    def eliminate(layer, carry):
        upper, r, f = carry
        lower = diff[layer]
        inv = 1.0 / (1.0 + lower + upper - upper * r)
        r, f = lower * inv, (moist[layer] + upper * f) * inv
        ratio[layer] = r
        moist[layer] = f
        return lower, r, f
    lower, _, bottom = lax.fori_loop(1, depth, eliminate, (e0, r0, f0))
    drain = lower * bottom
    hot = one_hot_rows(tile_ref[...], offset_ref[...], count_ref[0], cols_n, tile_rows)
    mine = jnp.dot(hot, drain, precision=lax.Precision.HIGHEST, preferred_element_type=jnp.float32)
    recharge[0, gy] = mine.reshape(cols_n, tile_rows, LANES)

    rech_copies = []
    n = 0
    for i, (dx, exists, _, rows) in enumerate(row_steps):
        source_row = None if dx == 0 else (has_above if dx == 1 else has_below)
        for dy in range(0 if dx else 1, cols_n):
            to = lax.rem(gy + dy, cols_n)
            came = lax.rem(gy + cols_n - dy, cols_n)
            def copy(slot, to=to, dx=dx, i=i, rows=rows, n=n):
                return pltpu.make_async_remote_copy(
                    src_ref=recharge.at[0, gy, :, rows],
                    dst_ref=recharge.at[i, slot, :, rows],
                    send_sem=rech_send.at[n],
                    recv_sem=rech_recv.at[n],
                    device_id=(gx + dx, to),
                    device_id_type=MESH,
                )
            rech_copies.append((exists, source_row, copy(gy), copy(came)))
            n += 1
    for exists, _, out, _ in rech_copies:
        when(exists, out.start)

    def substitute(i, wet):
        layer = depth - 2 - i
        wet = moist[layer] + ratio[layer] * wet
        moist[layer] = wet
        return wet
    lax.fori_loop(0, depth - 1, substitute, bottom)
    wet_copy = pltpu.make_async_copy(moist, wet_out, out_sem.at[0])
    wet_copy.start()

    ring_row = lax.broadcasted_iota(jnp.int32, (ring_rows, ring_cols), 0)
    ring_col = lax.broadcasted_iota(jnp.int32, (ring_rows, ring_cols), 1)
    row_ok = (ring_row < tile_rows) | ((ring_row < tile_rows + HALO) & has_below) | ((ring_row >= tile_rows + HALO) & has_above)
    col_ok = (ring_col < LANES) | ((ring_col < LANES + LANES // 2) & has_right) | ((ring_col >= LANES + LANES // 2) & has_left)
    mask = (row_ok & col_ok).astype(jnp.float32)
    on_grid = mask > 0.0

    for _, source, copy in row_copies + pack_copies:
        when(source, copy.wait_recv)

    side_on_grid = on_grid[:, LANES:]
    for g in range(groups):
        for f, dst in enumerate((h, k)):
            comb = jnp.where((lane % SLOT) < HALO, land_l[f, g], land_r[f, g])
            for s in range(min(per, nz - g * per)):
                side = pltpu.roll(comb, (LANES - HALO - SLOT * s) % LANES, 1)
                dst[1 + g * per + s, :, LANES:] = jnp.where(side_on_grid, side, 0.0)

    scale = 0.5 * flow_rate
    masked = scale * mask

    def east(x):
        return pltpu.roll(x, ring_cols - 1, 1)

    def west(x):
        return pltpu.roll(x, 1, 1)

    def south(x):
        return pltpu.roll(x, ring_rows - 1, 0)

    def north(x):
        return pltpu.roll(x, 1, 0)

    w_v[0] = empty

    def weights(block, _):
        z0 = block * BLOCK
        here = k[z0 + 1]
        up = jnp.where(z0 > 0, scale, 0.0) * (k[z0] + here)
        for j in range(BLOCK):
            z = z0 + j
            after = k[z + 2]
            down = jnp.where(z < nz - 1, scale, 0.0) * (here + after)
            parts = [masked * (here + turn(here)) for turn in (east, west, south, north)]
            for ref, part in zip((w_e, w_w, w_s, w_n), parts):
                ref[z] = part
            w_v[z + 1] = down
            w_d[z] = 1.0 - ((parts[0] + parts[1]) + (parts[2] + parts[3]) + (up + down))
            here, up = after, down
        return 0
    lax.fori_loop(0, nz // BLOCK, weights, 0)

    def step(src, z0, count):
        before, here = src[z0], src[z0 + 1]
        out = []
        for j in range(count):
            z = z0 + j
            after = src[z + 2]
            out.append(
                (w_d[z] * here + w_e[z] * east(here))
                + (w_w[z] * west(here) + w_s[z] * south(here))
                + (w_n[z] * north(here) + (w_v[z] * before + w_v[z + 1] * after))
            )
            before, here = here, after
        return out

    def sweep(src, dst, last):
        def body(block, _):
            z0 = block * BLOCK
            for j, new in enumerate(step(src, z0, BLOCK)):
                if last:
                    field[z0 + j] = new[0:tile_rows, 0:LANES]
                else:
                    dst[z0 + j + 1] = new
            return 0
        lax.fori_loop(0, nz // BLOCK, body, 0)

    for n in range(SWEEPS):
        src, dst = (h, h2) if n % 2 == 0 else (h2, h)
        sweep(src, dst, n == SWEEPS - 1)

    for _, source, _, arrived in rech_copies:
        when(source, arrived.wait_recv)

    def tile_sum(tile):
        parts = []
        for i, rows in ((0, whole), (1, last), (2, first)):
            total = recharge[i, 0, tile, rows]
            for s in range(1, cols_n):
                total = total + recharge[i, s, tile, rows]
            parts.append(total)
        return jnp.concatenate([parts[0], parts[2], parts[1]], axis=0)
    centre = tile_sum(gy)
    right = tile_sum(jnp.minimum(gy + 1, cols_n - 1))
    left = tile_sum(jnp.maximum(gy - 1, 0))
    side = jnp.where(lane < LANES // 2, right, left)
    for z in range(SWEEPS + 3):
        delta[z] = empty
        delta2[z] = empty
    delta[1] = jnp.where(on_grid, jnp.concatenate([centre, side], axis=1), 0.0)
    for n in range(SWEEPS):
        src, dst = (delta, delta2) if n % 2 == 0 else (delta2, delta)
        for z, new in enumerate(step(src, 0, min(n + 2, nz))):
            if n < SWEEPS - 1:
                dst[z + 1] = new
            else:
                field[z] = field[z] + new[0:tile_rows, 0:LANES]

    surf[gy] = field[0]
    surf_copies = []
    for dy in range(1, cols_n):
        to = lax.rem(gy + dy, cols_n)
        came = lax.rem(gy + cols_n - dy, cols_n)
        pair = [
            pltpu.make_async_remote_copy(
                src_ref=surf.at[gy],
                dst_ref=surf.at[slot],
                send_sem=surf_send.at[dy - 1],
                recv_sem=surf_recv.at[dy - 1],
                device_id=(gx, to),
                device_id_type=MESH,
            )
            for slot in (gy, came)
        ]
        pair[0].start()
        surf_copies.append(pair)
    field_copy = pltpu.make_async_copy(field, field_out, out_sem.at[1])
    field_copy.start()
    for _, arrived in surf_copies:
        arrived.wait_recv()
    surf_copy = pltpu.make_async_copy(surf, surf_out, out_sem.at[2])
    surf_copy.start()

    for exists, _, copy in row_copies + pack_copies:
        when(exists, copy.wait_send)
    for exists, _, out, _ in rech_copies:
        when(exists, out.wait_send)
    for out, _ in surf_copies:
        out.wait_send()
    wet_copy.wait()
    field_copy.wait()
    surf_copy.wait()


def exchange_kernel(
    tile_rows, cols_n,
    field_in, wet_in, surf_in, tile_in, offset_in, patch_in, count_ref,
    head_out, moist_out, patch_out,
    field, wet, surf, tile_ref, offset_ref, patch_ref, sem,
):
    depth, blocks, _ = wet.shape
    upper = pl.ds(0, depth - 1)
    loads = [
        pltpu.make_async_copy(src, dst, sem.at[i])
        for i, (src, dst) in enumerate((
            (tile_in, tile_ref),
            (offset_in, offset_ref),
            (patch_in, patch_ref),
            (surf_in, surf),
            (wet_in.at[depth - 1], wet.at[depth - 1]),
            (wet_in.at[upper], wet.at[upper]),
            (field_in, field),
        ))
    ]
    for copy in loads:
        copy.start()
    for copy in loads[:5]:
        copy.wait()
    hot = one_hot_rows(tile_ref[...], offset_ref[...], count_ref[0], cols_n, tile_rows)
    surface = surf[...].reshape(cols_n * tile_rows, LANES)
    saturation = lax.dot_general(
        hot, surface, (((0,), (0,)), ((), ())),
        precision=lax.Precision.HIGHEST, preferred_element_type=jnp.float32,
    )
    patch = lax.broadcasted_iota(jnp.int32, (PATCH_DEV, blocks), 0)
    patch_hot = (patch == patch_ref[...]).astype(jnp.float32)
    patch_out[...] = jnp.dot(
        patch_hot, saturation, precision=lax.Precision.HIGHEST, preferred_element_type=jnp.float32
    )
    used = (lax.broadcasted_iota(jnp.int32, (blocks, LANES), 0) < count_ref[0]).astype(jnp.float32)
    wet_bottom = wet[depth - 1]
    wet[depth - 1] = wet_bottom + capillary * (saturation - used * wet_bottom)
    stores = [
        pltpu.make_async_copy(wet.at[depth - 1], moist_out.at[depth - 1], sem.at[0]),
        pltpu.make_async_copy(wet.at[upper], moist_out.at[upper], sem.at[1]),
        pltpu.make_async_copy(field, head_out, sem.at[2]),
    ]
    stores[0].start()
    for load, store in zip(loads[5:], stores[1:]):
        load.wait()
        store.start()
    for store in stores:
        store.wait()


def local(rows_n, cols_n, moisture, diffusivity, rain, head, conductivity, tile_ids, offsets, patch_ids, counts):
    blocks, depth, _ = moisture.shape
    nz, tile_rows, _ = head.shape
    moisture = jnp.transpose(moisture, (1, 0, 2))
    diffusivity = jnp.transpose(diffusivity, (1, 0, 2))
    tile_ids, offsets, patch_ids = (x.reshape(1, blocks) for x in (tile_ids, offsets, patch_ids))
    f32 = jnp.float32
    per = LANES // SLOT
    groups = pl.cdiv(nz, per)
    ring = (tile_rows + 2 * HALO, 2 * LANES)
    hbm = pl.BlockSpec(memory_space=pltpu.HBM)
    vmem = pl.BlockSpec(memory_space=pltpu.VMEM)
    smem = pl.BlockSpec(memory_space=pltpu.SMEM)
    dma = pltpu.SemaphoreType.DMA
    rech = 3 * cols_n - 1
    field, wet, surf = pl.pallas_call(
        functools.partial(flow_kernel, (rows_n, cols_n, nz, tile_rows)),
        name="flow",
        out_shape=(
            jax.ShapeDtypeStruct((nz, tile_rows, LANES), f32),
            jax.ShapeDtypeStruct((depth, blocks, LANES), f32),
            jax.ShapeDtypeStruct((cols_n, tile_rows, LANES), f32),
        ),
        in_specs=[hbm] * 7 + [smem],
        out_specs=(hbm,) * 3,
        scratch_shapes=[
            pltpu.VMEM((nz + 2,) + ring, f32),
            pltpu.VMEM((nz + 2,) + ring, f32),
            pltpu.VMEM((nz + 2,) + ring, f32),
            pltpu.VMEM((nz, tile_rows, LANES), f32),
            pltpu.VMEM((nz,) + ring, f32),
            pltpu.VMEM((nz,) + ring, f32),
            pltpu.VMEM((nz,) + ring, f32),
            pltpu.VMEM((nz,) + ring, f32),
            pltpu.VMEM((nz,) + ring, f32),
            pltpu.VMEM((nz + 1,) + ring, f32),
            pltpu.VMEM((SWEEPS + 3,) + ring, f32),
            pltpu.VMEM((SWEEPS + 3,) + ring, f32),
            pltpu.VMEM((2, groups, tile_rows, LANES), f32),
            pltpu.VMEM((2, groups, ring[0], LANES), f32),
            pltpu.VMEM((2, groups, ring[0], LANES), f32),
            pltpu.VMEM((depth, blocks, LANES), f32),
            pltpu.VMEM((depth, blocks, LANES), f32),
            pltpu.VMEM((depth, blocks, LANES), f32),
            pltpu.VMEM((blocks, LANES), f32),
            pltpu.VMEM((1, blocks), jnp.int32),
            pltpu.VMEM((1, blocks), jnp.int32),
            pltpu.VMEM((3, cols_n, cols_n, tile_rows, LANES), f32),
            pltpu.VMEM((cols_n, tile_rows, LANES), f32),
            dma((7,)), dma((3,)), dma((4,)), dma((4,)), dma((6,)), dma((6,)),
            dma((rech,)), dma((rech,)), dma((cols_n,)), dma((cols_n,)),
        ],
        compiler_params=pltpu.CompilerParams(
            collective_id=0, has_side_effects=True, vmem_limit_bytes=63 * 1024 * 1024
        ),
    )(moisture, diffusivity, rain, head, conductivity, tile_ids, offsets, counts)
    head_out, moist_out, patch_sums = pl.pallas_call(
        functools.partial(exchange_kernel, tile_rows, cols_n),
        name="exchange",
        out_shape=(
            jax.ShapeDtypeStruct((nz, tile_rows, LANES), f32),
            jax.ShapeDtypeStruct((depth, blocks, LANES), f32),
            jax.ShapeDtypeStruct((PATCH_DEV, LANES), f32),
        ),
        in_specs=[hbm] * 6 + [smem],
        out_specs=(hbm, hbm, vmem),
        scratch_shapes=[
            pltpu.VMEM((nz, tile_rows, LANES), f32),
            pltpu.VMEM((depth, blocks, LANES), f32),
            pltpu.VMEM((cols_n, tile_rows, LANES), f32),
            pltpu.VMEM((1, blocks), jnp.int32),
            pltpu.VMEM((1, blocks), jnp.int32),
            pltpu.VMEM((1, blocks), jnp.int32),
            dma((7,)),
        ],
        compiler_params=pltpu.CompilerParams(vmem_limit_bytes=63 * 1024 * 1024),
    )(field, wet, surf, tile_ids, offsets, patch_ids, counts)
    return head_out, jnp.transpose(moist_out, (1, 0, 2)), patch_sums


def solution(mesh):
    placed = (
        P(("gx", "gy"), None, None),
        P(("gx", "gy"), None, None),
        P(("gx", "gy"), None),
        P(None, "gx", "gy"),
        P(None, "gx", "gy"),
        P(("gx", "gy")),
        P(("gx", "gy")),
        P(("gx", "gy")),
        P(("gx", "gy")),
    )
    return jax.shard_map(
        functools.partial(local, mesh.shape["gx"], mesh.shape["gy"]),
        mesh=mesh,
        in_specs=placed,
        out_specs=(P(None, "gx", "gy"), P(("gx", "gy"), None, None), P(("gx", "gy"), None)),
        check_vma=False,
    )
```

```python
import functools

import jax
import jax.numpy as jnp
from jax import lax
from jax.experimental import pallas as pl
from jax.experimental.pallas import tpu as pltpu
from jax.sharding import PartitionSpec as P

PATCH_DEV = 8
SWEEPS = 6
HALO = 8
BLOCK = 5
CHUNK = 2 * BLOCK
PAD = 8
SLOT = 2 * HALO
LANES = 128
MESH = pl.DeviceIdType.MESH

flow_rate = 0.15
capillary = 0.5


def one_hot_rows(tile, offset, used_count, tile_count, tile_rows):
    blocks = tile.shape[1]
    block = lax.broadcasted_iota(jnp.int32, (1, blocks), 1)
    target = jnp.where(block < used_count, tile * tile_rows + offset, -1)
    slot = lax.broadcasted_iota(jnp.int32, (tile_count * tile_rows, blocks), 0)
    return (slot == target).astype(jnp.float32)


def flow_kernel(
    sizes,
    moist_in, diff_in, rain_in, head_in, cond_in, tile_in, offset_in, count_ref,
    field_out, wet_out, surf_out,
    h, h2, k, field, w_d, w_e, w_w, w_s, w_n, w_v, delta, delta2, packed, land_l, land_r, moist, diff, ratio, rain,
    tile_ref, offset_ref, recharge, surf,
    local_sem, out_sem, row_send, row_recv, pack_send, pack_recv, rech_send, rech_recv,
    surf_send, surf_recv,
):
    rows_n, cols_n, nz, tile_rows = sizes
    gx, gy = lax.axis_index("gx"), lax.axis_index("gy")
    has_below, has_above = gx < rows_n - 1, gx > 0
    has_right, has_left = gy < cols_n - 1, gy > 0
    depth = moist.shape[0]
    groups = packed.shape[1]
    ring_rows, ring_cols = h.shape[1], h.shape[2]
    below = pl.ds(tile_rows, HALO)
    above = pl.ds(tile_rows + HALO, HALO)
    first = pl.ds(0, HALO)
    last = pl.ds(tile_rows - HALO, HALO)
    whole = pl.ds(0, tile_rows)
    main = pl.ds(0, LANES)
    layers = pl.ds(PAD, nz)
    chunks = nz // CHUNK

    local = [
        pltpu.make_async_copy(src, dst, local_sem.at[i])
        for i, (src, dst) in enumerate((
            (head_in, h.at[layers, whole, main]),
            (cond_in, k.at[layers, whole, main]),
            (moist_in, moist),
            (diff_in, diff),
            (rain_in, rain),
            (tile_in, tile_ref),
            (offset_in, offset_ref),
        ))
    ]
    for copy in local:
        copy.start()

    row_steps = ((0, None, whole, whole), (1, has_below, above, last), (-1, has_above, below, first))
    peers = []
    for dx, exists, _, _ in row_steps:
        for dy in range(cols_n):
            if dx or dy:
                peers.append((dx, exists, lax.rem(gy + dy, cols_n)))

    def when(cond, body):
        if cond is None:
            body()
        else:
            pl.when(cond)(body)

    def both(a, b):
        return b if a is None else jnp.logical_and(a, b)

    empty = jnp.zeros((ring_rows, ring_cols), jnp.float32)
    for z in range(PAD):
        for ref in (h, h2, k, w_d, w_e, w_w, w_s, w_n, w_v):
            ref[z] = empty
        for ref in (h, h2, k):
            ref[PAD + nz + z] = empty

    def clear(rows):
        def body(z, _):
            for ref in (h, k):
                ref[z, rows, main] = jnp.zeros((HALO, LANES), jnp.float32)
            return 0
        lax.fori_loop(PAD, PAD + nz, body, 0)
    pl.when(gx == 0)(lambda: clear(above))
    pl.when(gx == rows_n - 1)(lambda: clear(below))

    barrier = pltpu.get_barrier_semaphore()
    for dx, exists, col in peers:
        def greet(dx=dx, col=col):
            pl.semaphore_signal(barrier, inc=1, device_id=(gx + dx, col), device_id_type=MESH)
        when(exists, greet)

    local[0].wait()
    local[1].wait()
    lane = lax.broadcasted_iota(jnp.int32, (1, LANES), 1)

    per = LANES // SLOT
    for g in range(groups):
        for f, src in enumerate((h, k)):
            total = jnp.zeros((tile_rows, LANES), jnp.float32)
            for s in range(min(per, nz - g * per)):
                edge = pltpu.roll(src[PAD + g * per + s, 0:tile_rows, 0:LANES], (HALO + SLOT * s) % LANES, 1)
                inside = (lane >= SLOT * s) & (lane < SLOT * (s + 1))
                total = jnp.where(inside, edge, total)
            packed[f, g] = total

    def row_copy(i, f, c):
        dx, _, ring, mine = row_steps[1 + i]
        src, dst = ((head_in, h), (cond_in, k))[f]
        return pltpu.make_async_remote_copy(
            src_ref=src.at[pl.ds(CHUNK * c, CHUNK), mine],
            dst_ref=dst.at[pl.ds(PAD + CHUNK * c, CHUNK), ring, main],
            send_sem=row_send.at[2 * i + f, c],
            recv_sem=row_recv.at[2 * i + f, c],
            device_id=(gx + dx, gy),
            device_id_type=MESH,
        )

    def each_row(cond_of, c, act):
        for i in range(2):
            def body(i=i):
                for f in (1, 0):
                    act(row_copy(i, f, c))
            pl.when(cond_of[i])(body)
    sends_row, gets_row = (has_below, has_above), (has_above, has_below)

    def start_rows(c, _):
        each_row(sends_row, c, lambda copy: copy.start())
        return 0

    def finish_rows(c, _):
        each_row(sends_row, c, lambda copy: copy.wait_send())
        return 0

    pack_copies = []
    n = 0
    for dx, exists, ring, mine in row_steps:
        source_row = None if dx == 0 else (has_above if dx == 1 else has_below)
        for dy, side, target, source in ((1, land_l, has_right, has_left), (-1, land_r, has_left, has_right)):
            pack_copies.append((both(exists, target), both(source_row, source), pltpu.make_async_remote_copy(
                src_ref=packed.at[:, :, mine],
                dst_ref=side.at[:, :, ring],
                send_sem=pack_send.at[n],
                recv_sem=pack_recv.at[n],
                device_id=(gx + dx, gy + dy),
                device_id_type=MESH,
            )))
            n += 1
    near_rows = 1 + has_below.astype(jnp.int32) + has_above.astype(jnp.int32)
    pl.semaphore_wait(barrier, cols_n * near_rows - 1)
    for exists, _, copy in pack_copies:
        when(exists, copy.start)
    lax.fori_loop(0, chunks, start_rows, 0)

    for copy in local[2:]:
        copy.wait()
    e0 = diff[0]
    inv = 1.0 / (1.0 + e0)
    r0, f0 = e0 * inv, (moist[0] + rain[...]) * inv
    ratio[0] = r0
    moist[0] = f0

    def eliminate(layer, carry):
        upper, r, f = carry
        lower = diff[layer]
        inv = 1.0 / (1.0 + lower + upper - upper * r)
        r, f = lower * inv, (moist[layer] + upper * f) * inv
        ratio[layer] = r
        moist[layer] = f
        return lower, r, f
    lower, _, bottom = lax.fori_loop(1, depth, eliminate, (e0, r0, f0))
    drain = lower * bottom
    hot = one_hot_rows(tile_ref[...], offset_ref[...], count_ref[0], cols_n, tile_rows)
    mine = jnp.dot(hot, drain, precision=lax.Precision.HIGHEST, preferred_element_type=jnp.float32)
    recharge[0, gy] = mine.reshape(cols_n, tile_rows, LANES)

    rech_copies = []
    n = 0
    for i, (dx, exists, _, rows) in enumerate(row_steps):
        source_row = None if dx == 0 else (has_above if dx == 1 else has_below)
        for dy in range(0 if dx else 1, cols_n):
            to = lax.rem(gy + dy, cols_n)
            came = lax.rem(gy + cols_n - dy, cols_n)
            def copy(slot, to=to, dx=dx, i=i, rows=rows, n=n):
                return pltpu.make_async_remote_copy(
                    src_ref=recharge.at[0, gy, :, rows],
                    dst_ref=recharge.at[i, slot, :, rows],
                    send_sem=rech_send.at[n],
                    recv_sem=rech_recv.at[n],
                    device_id=(gx + dx, to),
                    device_id_type=MESH,
                )
            rech_copies.append((exists, source_row, copy(gy), copy(came)))
            n += 1
    for exists, _, out, _ in rech_copies:
        when(exists, out.start)

    def substitute(i, wet):
        layer = depth - 2 - i
        wet = moist[layer] + ratio[layer] * wet
        moist[layer] = wet
        return wet
    lax.fori_loop(0, depth - 1, substitute, bottom)
    wet_copy = pltpu.make_async_copy(moist, wet_out, out_sem.at[0])
    wet_copy.start()

    ring_row = lax.broadcasted_iota(jnp.int32, (ring_rows, ring_cols), 0)
    ring_col = lax.broadcasted_iota(jnp.int32, (ring_rows, ring_cols), 1)
    row_ok = (ring_row < tile_rows) | ((ring_row < tile_rows + HALO) & has_below) | ((ring_row >= tile_rows + HALO) & has_above)
    col_ok = (ring_col < LANES) | ((ring_col < LANES + LANES // 2) & has_right) | ((ring_col >= LANES + LANES // 2) & has_left)
    mask = (row_ok & col_ok).astype(jnp.float32)
    on_grid = mask > 0.0

    for _, source, copy in pack_copies:
        when(source, copy.wait_recv)

    side_on_grid = on_grid[:, LANES:]
    for g in range(groups):
        for f, dst in enumerate((h, k)):
            comb = jnp.where((lane % SLOT) < HALO, land_l[f, g], land_r[f, g])
            for s in range(min(per, nz - g * per)):
                side = pltpu.roll(comb, (LANES - HALO - SLOT * s) % LANES, 1)
                dst[PAD + g * per + s, :, LANES:] = jnp.where(side_on_grid, side, 0.0)

    scale = 0.5 * flow_rate
    masked = scale * mask

    def east(x):
        return pltpu.roll(x, ring_cols - 1, 1)

    def west(x):
        return pltpu.roll(x, 1, 1)

    def south(x):
        return pltpu.roll(x, ring_rows - 1, 0)

    def north(x):
        return pltpu.roll(x, 1, 0)

    def weights(z0):
        here = k[PAD + z0]
        up = jnp.where((z0 > 0) & (z0 < nz), scale, 0.0) * (k[PAD + z0 - 1] + here)
        for j in range(BLOCK):
            z = z0 + j
            at = PAD + z
            after = k[at + 1]
            down = jnp.where((z >= 0) & (z < nz - 1), scale, 0.0) * (here + after)
            parts = [masked * (here + turn(here)) for turn in (east, west, south, north)]
            for ref, part in zip((w_e, w_w, w_s, w_n), parts):
                ref[at] = part
            w_v[at + 1] = down
            w_d[at] = 1.0 - ((parts[0] + parts[1]) + (parts[2] + parts[3]) + (up + down))
            here, up = after, down

    def step(src, at, w_at, count):
        before, here = src[at - 1], src[at]
        out = []
        for j in range(count):
            w = w_at + j
            after = src[at + j + 1]
            out.append(
                (w_d[w] * here + w_e[w] * east(here))
                + (w_w[w] * west(here) + w_s[w] * south(here))
                + (w_n[w] * north(here) + (w_v[w] * before + w_v[w + 1] * after))
            )
            before, here = here, after
        return out

    def sweep(n, z0):
        src, dst = (h, h2) if n % 2 == 0 else (h2, h)
        for j, new in enumerate(step(src, PAD + z0, PAD + z0, BLOCK)):
            if n < SWEEPS - 1:
                dst[PAD + z0 + j] = new
            else:
                field[PAD + z0 + j] = new[0:tile_rows, 0:LANES]

    def wave(c, _):
        @pl.when(c < chunks)
        def _():
            each_row(gets_row, c, lambda copy: copy.wait_recv())

        def run(start, work):
            begin = jnp.where(start + BLOCK <= 0, 1, 0)
            end = jnp.where(start + BLOCK >= nz, 1, 2)
            def body(b, _):
                work(start + BLOCK * b)
                return 0
            lax.fori_loop(begin, end, body, 0)
        run(CHUNK * c - 1, weights)
        for n in range(SWEEPS):
            run(CHUNK * c - (n + 1), functools.partial(sweep, n))
        return 0
    lax.fori_loop(0, chunks + 1, wave, 0)

    for _, source, _, arrived in rech_copies:
        when(source, arrived.wait_recv)

    def tile_sum(tile):
        parts = []
        for i, rows in ((0, whole), (1, last), (2, first)):
            total = recharge[i, 0, tile, rows]
            for s in range(1, cols_n):
                total = total + recharge[i, s, tile, rows]
            parts.append(total)
        return jnp.concatenate([parts[0], parts[2], parts[1]], axis=0)
    centre = tile_sum(gy)
    right = tile_sum(jnp.minimum(gy + 1, cols_n - 1))
    left = tile_sum(jnp.maximum(gy - 1, 0))
    side = jnp.where(lane < LANES // 2, right, left)
    for z in range(SWEEPS + 3):
        delta[z] = empty
        delta2[z] = empty
    delta[1] = jnp.where(on_grid, jnp.concatenate([centre, side], axis=1), 0.0)
    for n in range(SWEEPS):
        src, dst = (delta, delta2) if n % 2 == 0 else (delta2, delta)
        for z, new in enumerate(step(src, 1, PAD, min(n + 2, nz))):
            if n < SWEEPS - 1:
                dst[z + 1] = new
            else:
                field[PAD + z] = field[PAD + z] + new[0:tile_rows, 0:LANES]

    surf[gy] = field[PAD]
    surf_copies = []
    for dy in range(1, cols_n):
        to = lax.rem(gy + dy, cols_n)
        came = lax.rem(gy + cols_n - dy, cols_n)
        pair = [
            pltpu.make_async_remote_copy(
                src_ref=surf.at[gy],
                dst_ref=surf.at[slot],
                send_sem=surf_send.at[dy - 1],
                recv_sem=surf_recv.at[dy - 1],
                device_id=(gx, to),
                device_id_type=MESH,
            )
            for slot in (gy, came)
        ]
        pair[0].start()
        surf_copies.append(pair)
    field_copy = pltpu.make_async_copy(field.at[layers], field_out, out_sem.at[1])
    field_copy.start()
    for _, arrived in surf_copies:
        arrived.wait_recv()
    surf_copy = pltpu.make_async_copy(surf, surf_out, out_sem.at[2])
    surf_copy.start()

    lax.fori_loop(0, chunks, finish_rows, 0)
    for exists, _, copy in pack_copies:
        when(exists, copy.wait_send)
    for exists, _, out, _ in rech_copies:
        when(exists, out.wait_send)
    for out, _ in surf_copies:
        out.wait_send()
    wet_copy.wait()
    field_copy.wait()
    surf_copy.wait()


def exchange_kernel(
    tile_rows, cols_n,
    field_in, wet_in, surf_in, tile_in, offset_in, patch_in, count_ref,
    head_out, moist_out, patch_out,
    field, wet, surf, tile_ref, offset_ref, patch_ref, sem,
):
    depth, blocks, _ = wet.shape
    upper = pl.ds(0, depth - 1)
    loads = [
        pltpu.make_async_copy(src, dst, sem.at[i])
        for i, (src, dst) in enumerate((
            (tile_in, tile_ref),
            (offset_in, offset_ref),
            (patch_in, patch_ref),
            (surf_in, surf),
            (wet_in.at[depth - 1], wet.at[depth - 1]),
            (wet_in.at[upper], wet.at[upper]),
            (field_in, field),
        ))
    ]
    for copy in loads:
        copy.start()
    for copy in loads[:5]:
        copy.wait()
    hot = one_hot_rows(tile_ref[...], offset_ref[...], count_ref[0], cols_n, tile_rows)
    surface = surf[...].reshape(cols_n * tile_rows, LANES)
    saturation = lax.dot_general(
        hot, surface, (((0,), (0,)), ((), ())),
        precision=lax.Precision.HIGHEST, preferred_element_type=jnp.float32,
    )
    patch = lax.broadcasted_iota(jnp.int32, (PATCH_DEV, blocks), 0)
    patch_hot = (patch == patch_ref[...]).astype(jnp.float32)
    patch_out[...] = jnp.dot(
        patch_hot, saturation, precision=lax.Precision.HIGHEST, preferred_element_type=jnp.float32
    )
    used = (lax.broadcasted_iota(jnp.int32, (blocks, LANES), 0) < count_ref[0]).astype(jnp.float32)
    wet_bottom = wet[depth - 1]
    wet[depth - 1] = wet_bottom + capillary * (saturation - used * wet_bottom)
    stores = [
        pltpu.make_async_copy(wet.at[depth - 1], moist_out.at[depth - 1], sem.at[0]),
        pltpu.make_async_copy(wet.at[upper], moist_out.at[upper], sem.at[1]),
        pltpu.make_async_copy(field, head_out, sem.at[2]),
    ]
    stores[0].start()
    for load, store in zip(loads[5:], stores[1:]):
        load.wait()
        store.start()
    for store in stores:
        store.wait()


def local(rows_n, cols_n, moisture, diffusivity, rain, head, conductivity, tile_ids, offsets, patch_ids, counts):
    blocks, depth, _ = moisture.shape
    nz, tile_rows, _ = head.shape
    moisture = jnp.transpose(moisture, (1, 0, 2))
    diffusivity = jnp.transpose(diffusivity, (1, 0, 2))
    tile_ids, offsets, patch_ids = (x.reshape(1, blocks) for x in (tile_ids, offsets, patch_ids))
    f32 = jnp.float32
    per = LANES // SLOT
    groups = pl.cdiv(nz, per)
    ring = (tile_rows + 2 * HALO, 2 * LANES)
    hbm = pl.BlockSpec(memory_space=pltpu.HBM)
    vmem = pl.BlockSpec(memory_space=pltpu.VMEM)
    smem = pl.BlockSpec(memory_space=pltpu.SMEM)
    dma = pltpu.SemaphoreType.DMA
    rech = 3 * cols_n - 1
    field, wet, surf = pl.pallas_call(
        functools.partial(flow_kernel, (rows_n, cols_n, nz, tile_rows)),
        name="flow",
        out_shape=(
            jax.ShapeDtypeStruct((nz, tile_rows, LANES), f32),
            jax.ShapeDtypeStruct((depth, blocks, LANES), f32),
            jax.ShapeDtypeStruct((cols_n, tile_rows, LANES), f32),
        ),
        in_specs=[hbm] * 7 + [smem],
        out_specs=(hbm,) * 3,
        scratch_shapes=[
            pltpu.VMEM((nz + 2 * PAD,) + ring, f32),
            pltpu.VMEM((nz + 2 * PAD,) + ring, f32),
            pltpu.VMEM((nz + 2 * PAD,) + ring, f32),
            pltpu.VMEM((nz + 2 * PAD, tile_rows, LANES), f32),
            pltpu.VMEM((nz + 2 * PAD,) + ring, f32),
            pltpu.VMEM((nz + 2 * PAD,) + ring, f32),
            pltpu.VMEM((nz + 2 * PAD,) + ring, f32),
            pltpu.VMEM((nz + 2 * PAD,) + ring, f32),
            pltpu.VMEM((nz + 2 * PAD,) + ring, f32),
            pltpu.VMEM((nz + 2 * PAD,) + ring, f32),
            pltpu.VMEM((SWEEPS + 3,) + ring, f32),
            pltpu.VMEM((SWEEPS + 3,) + ring, f32),
            pltpu.VMEM((2, groups, tile_rows, LANES), f32),
            pltpu.VMEM((2, groups, ring[0], LANES), f32),
            pltpu.VMEM((2, groups, ring[0], LANES), f32),
            pltpu.VMEM((depth, blocks, LANES), f32),
            pltpu.VMEM((depth, blocks, LANES), f32),
            pltpu.VMEM((depth, blocks, LANES), f32),
            pltpu.VMEM((blocks, LANES), f32),
            pltpu.VMEM((1, blocks), jnp.int32),
            pltpu.VMEM((1, blocks), jnp.int32),
            pltpu.VMEM((3, cols_n, cols_n, tile_rows, LANES), f32),
            pltpu.VMEM((cols_n, tile_rows, LANES), f32),
            dma((7,)), dma((3,)), dma((4, nz // CHUNK)), dma((4, nz // CHUNK)), dma((6,)), dma((6,)),
            dma((rech,)), dma((rech,)), dma((cols_n,)), dma((cols_n,)),
        ],
        compiler_params=pltpu.CompilerParams(
            collective_id=0, has_side_effects=True, vmem_limit_bytes=63 * 1024 * 1024
        ),
    )(moisture, diffusivity, rain, head, conductivity, tile_ids, offsets, counts)
    head_out, moist_out, patch_sums = pl.pallas_call(
        functools.partial(exchange_kernel, tile_rows, cols_n),
        name="exchange",
        out_shape=(
            jax.ShapeDtypeStruct((nz, tile_rows, LANES), f32),
            jax.ShapeDtypeStruct((depth, blocks, LANES), f32),
            jax.ShapeDtypeStruct((PATCH_DEV, LANES), f32),
        ),
        in_specs=[hbm] * 6 + [smem],
        out_specs=(hbm, hbm, vmem),
        scratch_shapes=[
            pltpu.VMEM((nz, tile_rows, LANES), f32),
            pltpu.VMEM((depth, blocks, LANES), f32),
            pltpu.VMEM((cols_n, tile_rows, LANES), f32),
            pltpu.VMEM((1, blocks), jnp.int32),
            pltpu.VMEM((1, blocks), jnp.int32),
            pltpu.VMEM((1, blocks), jnp.int32),
            dma((7,)),
        ],
        compiler_params=pltpu.CompilerParams(vmem_limit_bytes=63 * 1024 * 1024),
    )(field, wet, surf, tile_ids, offsets, patch_ids, counts)
    return head_out, jnp.transpose(moist_out, (1, 0, 2)), patch_sums


def solution(mesh):
    placed = (
        P(("gx", "gy"), None, None),
        P(("gx", "gy"), None, None),
        P(("gx", "gy"), None),
        P(None, "gx", "gy"),
        P(None, "gx", "gy"),
        P(("gx", "gy")),
        P(("gx", "gy")),
        P(("gx", "gy")),
        P(("gx", "gy")),
    )
    return jax.shard_map(
        functools.partial(local, mesh.shape["gx"], mesh.shape["gy"]),
        mesh=mesh,
        in_specs=placed,
        out_specs=(P(None, "gx", "gy"), P(("gx", "gy"), None, None), P(("gx", "gy"), None)),
        check_vma=False,
    )
```

```python
import functools

import jax
import jax.numpy as jnp
from jax import lax
from jax.experimental import pallas as pl
from jax.experimental.pallas import tpu as pltpu
from jax.sharding import PartitionSpec as P

PATCH_DEV = 8
SWEEPS = 6
HALO = 8
BLOCK = 5
CHUNK = 2 * BLOCK
PAD = 8
SLOT = 2 * HALO
LANES = 128
MESH = pl.DeviceIdType.MESH

flow_rate = 0.15
capillary = 0.5


def one_hot_rows(tile, offset, used_count, tile_count, tile_rows):
    blocks = tile.shape[1]
    block = lax.broadcasted_iota(jnp.int32, (1, blocks), 1)
    target = jnp.where(block < used_count, tile * tile_rows + offset, -1)
    slot = lax.broadcasted_iota(jnp.int32, (tile_count * tile_rows, blocks), 0)
    return (slot == target).astype(jnp.float32)


def flow_kernel(
    sizes,
    moist_in, diff_in, rain_in, head_in, cond_in, tile_in, offset_in, count_ref,
    field_out, wet_out, surf_out,
    h_land, k_land, spread, h, h2, k, field, w_d, w_e, w_w, w_s, w_n, w_v, delta, delta2, packed, land_l, land_r, moist, diff, ratio, rain,
    tile_ref, offset_ref, recharge, surf,
    local_sem, out_sem, row_send, row_recv, pack_send, pack_recv, rech_send, rech_recv,
    surf_send, surf_recv,
):
    rows_n, cols_n, nz, tile_rows = sizes
    gx, gy = lax.axis_index("gx"), lax.axis_index("gy")
    has_below, has_above = gx < rows_n - 1, gx > 0
    has_right, has_left = gy < cols_n - 1, gy > 0
    depth = moist.shape[0]
    groups = packed.shape[1]
    ring_rows, ring_cols = h.shape[1], h.shape[2]
    below = pl.ds(tile_rows, HALO)
    above = pl.ds(tile_rows + HALO, HALO)
    first = pl.ds(0, HALO)
    last = pl.ds(tile_rows - HALO, HALO)
    whole = pl.ds(0, tile_rows)
    layers = pl.ds(PAD, nz)
    chunks = nz // CHUNK

    local = [
        pltpu.make_async_copy(src, dst, local_sem.at[i])
        for i, (src, dst) in enumerate((
            (head_in, h_land.at[:, whole]),
            (cond_in, k_land.at[:, whole]),
            (moist_in, moist),
            (diff_in, diff),
            (rain_in, rain),
            (tile_in, tile_ref),
            (offset_in, offset_ref),
        ))
    ]
    for copy in local:
        copy.start()

    row_steps = ((0, None, whole, whole), (1, has_below, above, last), (-1, has_above, below, first))
    peers = []
    for dx, exists, _, _ in row_steps:
        for dy in range(cols_n):
            if dx or dy:
                peers.append((dx, exists, lax.rem(gy + dy, cols_n)))

    def when(cond, body):
        if cond is None:
            body()
        else:
            pl.when(cond)(body)

    def both(a, b):
        return b if a is None else jnp.logical_and(a, b)

    empty = jnp.zeros((ring_rows, ring_cols), jnp.float32)
    for z in range(PAD):
        for ref in (h, h2, k, w_d, w_e, w_w, w_s, w_n, w_v):
            ref[z] = empty
        for ref in (h, h2, k):
            ref[PAD + nz + z] = empty

    def clear(rows):
        def body(z, _):
            for ref in (h_land, k_land):
                ref[z, rows] = jnp.zeros((HALO, LANES), jnp.float32)
            return 0
        lax.fori_loop(0, nz, body, 0)
    pl.when(gx == 0)(lambda: clear(above))
    pl.when(gx == rows_n - 1)(lambda: clear(below))

    barrier = pltpu.get_barrier_semaphore()
    for dx, exists, col in peers:
        def greet(dx=dx, col=col):
            pl.semaphore_signal(barrier, inc=1, device_id=(gx + dx, col), device_id_type=MESH)
        when(exists, greet)

    local[0].wait()
    local[1].wait()
    lane = lax.broadcasted_iota(jnp.int32, (1, LANES), 1)

    per = LANES // SLOT
    for g in range(groups):
        for f, src in enumerate((h_land, k_land)):
            total = jnp.zeros((tile_rows, LANES), jnp.float32)
            for s in range(min(per, nz - g * per)):
                edge = pltpu.roll(src[g * per + s, 0:tile_rows], (HALO + SLOT * s) % LANES, 1)
                inside = (lane >= SLOT * s) & (lane < SLOT * (s + 1))
                total = jnp.where(inside, edge, total)
            packed[f, g] = total

    def row_copy(i, f, c):
        dx, _, ring, mine = row_steps[1 + i]
        src, dst = ((head_in, h_land), (cond_in, k_land))[f]
        return pltpu.make_async_remote_copy(
            src_ref=src.at[pl.ds(CHUNK * c, CHUNK), mine],
            dst_ref=dst.at[pl.ds(CHUNK * c, CHUNK), ring],
            send_sem=row_send.at[2 * i + f, c],
            recv_sem=row_recv.at[2 * i + f, c],
            device_id=(gx + dx, gy),
            device_id_type=MESH,
        )

    def each_row(cond_of, c, act):
        for i in range(2):
            def body(i=i):
                for f in (1, 0):
                    act(row_copy(i, f, c))
            pl.when(cond_of[i])(body)
    sends_row, gets_row = (has_below, has_above), (has_above, has_below)

    def start_rows(c, _):
        each_row(sends_row, c, lambda copy: copy.start())
        return 0

    def finish_rows(c, _):
        each_row(sends_row, c, lambda copy: copy.wait_send())
        return 0

    pack_copies = []
    n = 0
    for dx, exists, ring, mine in row_steps:
        source_row = None if dx == 0 else (has_above if dx == 1 else has_below)
        for dy, side, target, source in ((1, land_l, has_right, has_left), (-1, land_r, has_left, has_right)):
            pack_copies.append((both(exists, target), both(source_row, source), pltpu.make_async_remote_copy(
                src_ref=packed.at[:, :, mine],
                dst_ref=side.at[:, :, ring],
                send_sem=pack_send.at[n],
                recv_sem=pack_recv.at[n],
                device_id=(gx + dx, gy + dy),
                device_id_type=MESH,
            )))
            n += 1
    near_rows = 1 + has_below.astype(jnp.int32) + has_above.astype(jnp.int32)
    pl.semaphore_wait(barrier, cols_n * near_rows - 1)
    for exists, _, copy in pack_copies:
        when(exists, copy.start)
    lax.fori_loop(0, chunks, start_rows, 0)

    for copy in local[2:]:
        copy.wait()
    e0 = diff[0]
    inv = 1.0 / (1.0 + e0)
    r0, f0 = e0 * inv, (moist[0] + rain[...]) * inv
    ratio[0] = r0
    moist[0] = f0

    def eliminate(layer, carry):
        upper, r, f = carry
        lower = diff[layer]
        inv = 1.0 / (1.0 + lower + upper - upper * r)
        r, f = lower * inv, (moist[layer] + upper * f) * inv
        ratio[layer] = r
        moist[layer] = f
        return lower, r, f
    lower, _, bottom = lax.fori_loop(1, depth, eliminate, (e0, r0, f0))
    drain = lower * bottom
    hot = one_hot_rows(tile_ref[...], offset_ref[...], count_ref[0], cols_n, tile_rows)
    mine = jnp.dot(hot, drain, precision=lax.Precision.HIGHEST, preferred_element_type=jnp.float32)
    recharge[0, gy] = mine.reshape(cols_n, tile_rows, LANES)

    rech_copies = []
    n = 0
    for i, (dx, exists, _, rows) in enumerate(row_steps):
        source_row = None if dx == 0 else (has_above if dx == 1 else has_below)
        for dy in range(0 if dx else 1, cols_n):
            to = lax.rem(gy + dy, cols_n)
            came = lax.rem(gy + cols_n - dy, cols_n)
            def copy(slot, to=to, dx=dx, i=i, rows=rows, n=n):
                return pltpu.make_async_remote_copy(
                    src_ref=recharge.at[0, gy, :, rows],
                    dst_ref=recharge.at[i, slot, :, rows],
                    send_sem=rech_send.at[n],
                    recv_sem=rech_recv.at[n],
                    device_id=(gx + dx, to),
                    device_id_type=MESH,
                )
            rech_copies.append((exists, source_row, copy(gy), copy(came)))
            n += 1
    for exists, _, out, _ in rech_copies:
        when(exists, out.start)

    def substitute(i, wet):
        layer = depth - 2 - i
        wet = moist[layer] + ratio[layer] * wet
        moist[layer] = wet
        return wet
    lax.fori_loop(0, depth - 1, substitute, bottom)
    wet_copy = pltpu.make_async_copy(moist, wet_out, out_sem.at[0])
    wet_copy.start()

    slabs = ring_rows // 8
    place = lax.broadcasted_iota(jnp.int32, (ring_rows, ring_cols), 0)
    ring_row = slabs * (place % 8) + place // 8
    ring_col = lax.broadcasted_iota(jnp.int32, (ring_rows, ring_cols), 1)
    row_ok = (ring_row < tile_rows) | ((ring_row < tile_rows + HALO) & has_below) | ((ring_row >= tile_rows + HALO) & has_above)
    col_ok = (ring_col < LANES) | ((ring_col < LANES + LANES // 2) & has_right) | ((ring_col >= LANES + LANES // 2) & has_left)
    mask = (row_ok & col_ok).astype(jnp.float32)
    on_grid = mask > 0.0

    for _, source, copy in pack_copies:
        when(source, copy.wait_recv)

    def interleaved(ref, *at):
        return jnp.concatenate([ref[(*at, pl.ds(i, 8, stride=slabs))] for i in range(slabs)], axis=0)

    side_on_grid = on_grid[:, LANES:]
    for g in range(groups):
        for f, dst in enumerate((h, k)):
            comb = jnp.where((lane % SLOT) < HALO, interleaved(land_l, f, g), interleaved(land_r, f, g))
            for s in range(min(per, nz - g * per)):
                side = pltpu.roll(comb, (LANES - HALO - SLOT * s) % LANES, 1)
                dst[PAD + g * per + s, :, LANES:] = jnp.where(side_on_grid, side, 0.0)

    scale = 0.5 * flow_rate
    masked = scale * mask

    def east(x):
        return pltpu.roll(x, ring_cols - 1, 1)

    def west(x):
        return pltpu.roll(x, 1, 1)

    def south(x):
        return jnp.concatenate([x[8:], pltpu.roll(x[:8], 7, 0)], axis=0)

    def north(x):
        return jnp.concatenate([pltpu.roll(x[-8:], 1, 0), x[:-8]], axis=0)

    def weights(z0):
        here = k[PAD + z0]
        up = jnp.where((z0 > 0) & (z0 < nz), scale, 0.0) * (k[PAD + z0 - 1] + here)
        for j in range(BLOCK):
            z = z0 + j
            at = PAD + z
            after = k[at + 1]
            down = jnp.where((z >= 0) & (z < nz - 1), scale, 0.0) * (here + after)
            parts = [masked * (here + turn(here)) for turn in (east, west, south, north)]
            for ref, part in zip((w_e, w_w, w_s, w_n), parts):
                ref[at] = part
            w_v[at + 1] = down
            w_d[at] = 1.0 - ((parts[0] + parts[1]) + (parts[2] + parts[3]) + (up + down))
            here, up = after, down

    def step(src, at, w_at, count):
        before, here = src[at - 1], src[at]
        out = []
        for j in range(count):
            w = w_at + j
            after = src[at + j + 1]
            out.append(
                (w_d[w] * here + w_e[w] * east(here))
                + (w_w[w] * west(here) + w_s[w] * south(here))
                + (w_n[w] * north(here) + (w_v[w] * before + w_v[w + 1] * after))
            )
            before, here = here, after
        return out

    tile_part = tile_rows // slabs

    def put_tile(at, new, add):
        for i in range(slabs):
            rows = pl.ds(i, tile_part, stride=slabs)
            part = new[8 * i : 8 * i + tile_part, 0:LANES]
            field[at, rows] = field[at, rows] + part if add else part

    def sweep(n, z0):
        src, dst = (h, h2) if n % 2 == 0 else (h2, h)
        for j, new in enumerate(step(src, PAD + z0, PAD + z0, BLOCK)):
            if n < SWEEPS - 1:
                dst[PAD + z0 + j] = new
            else:
                put_tile(PAD + z0 + j, new, False)

    def wave(c, _):
        @pl.when(c < chunks)
        def _():
            each_row(gets_row, c, lambda copy: copy.wait_recv())
            for j in range(CHUNK):
                z = CHUNK * c + j
                for src, dst in ((h_land, h), (k_land, k)):
                    dst[PAD + z, :, 0:LANES] = interleaved(src, z)

        def run(start, work):
            begin = jnp.where(start + BLOCK <= 0, 1, 0)
            end = jnp.where(start + BLOCK >= nz, 1, 2)
            def body(b, _):
                work(start + BLOCK * b)
                return 0
            lax.fori_loop(begin, end, body, 0)
        run(CHUNK * c - 1, weights)
        for n in range(SWEEPS):
            run(CHUNK * c - (n + 1), functools.partial(sweep, n))
        return 0
    lax.fori_loop(0, chunks + 1, wave, 0)

    for _, source, _, arrived in rech_copies:
        when(source, arrived.wait_recv)

    def tile_sum(tile):
        parts = []
        for i, rows in ((0, whole), (1, last), (2, first)):
            total = recharge[i, 0, tile, rows]
            for s in range(1, cols_n):
                total = total + recharge[i, s, tile, rows]
            parts.append(total)
        return jnp.concatenate([parts[0], parts[2], parts[1]], axis=0)
    centre = tile_sum(gy)
    right = tile_sum(jnp.minimum(gy + 1, cols_n - 1))
    left = tile_sum(jnp.maximum(gy - 1, 0))
    side = jnp.where(lane < LANES // 2, right, left)
    for z in range(SWEEPS + 3):
        delta[z] = empty
        delta2[z] = empty
    spread[0] = centre
    spread[1] = side
    start = jnp.concatenate([interleaved(spread, 0), interleaved(spread, 1)], axis=1)
    delta[1] = jnp.where(on_grid, start, 0.0)
    for n in range(SWEEPS):
        src, dst = (delta, delta2) if n % 2 == 0 else (delta2, delta)
        for z, new in enumerate(step(src, 1, PAD, min(n + 2, nz))):
            if n < SWEEPS - 1:
                dst[z + 1] = new
            else:
                put_tile(PAD + z, new, True)

    surf[gy] = field[PAD]
    surf_copies = []
    for dy in range(1, cols_n):
        to = lax.rem(gy + dy, cols_n)
        came = lax.rem(gy + cols_n - dy, cols_n)
        pair = [
            pltpu.make_async_remote_copy(
                src_ref=surf.at[gy],
                dst_ref=surf.at[slot],
                send_sem=surf_send.at[dy - 1],
                recv_sem=surf_recv.at[dy - 1],
                device_id=(gx, to),
                device_id_type=MESH,
            )
            for slot in (gy, came)
        ]
        pair[0].start()
        surf_copies.append(pair)
    field_copy = pltpu.make_async_copy(field.at[layers], field_out, out_sem.at[1])
    field_copy.start()
    for _, arrived in surf_copies:
        arrived.wait_recv()
    surf_copy = pltpu.make_async_copy(surf, surf_out, out_sem.at[2])
    surf_copy.start()

    lax.fori_loop(0, chunks, finish_rows, 0)
    for exists, _, copy in pack_copies:
        when(exists, copy.wait_send)
    for exists, _, out, _ in rech_copies:
        when(exists, out.wait_send)
    for out, _ in surf_copies:
        out.wait_send()
    wet_copy.wait()
    field_copy.wait()
    surf_copy.wait()


def exchange_kernel(
    tile_rows, cols_n,
    field_in, wet_in, surf_in, tile_in, offset_in, patch_in, count_ref,
    head_out, moist_out, patch_out,
    field, wet, surf, tile_ref, offset_ref, patch_ref, sem,
):
    depth, blocks, _ = wet.shape
    upper = pl.ds(0, depth - 1)
    loads = [
        pltpu.make_async_copy(src, dst, sem.at[i])
        for i, (src, dst) in enumerate((
            (tile_in, tile_ref),
            (offset_in, offset_ref),
            (patch_in, patch_ref),
            (surf_in, surf),
            (wet_in.at[depth - 1], wet.at[depth - 1]),
            (wet_in.at[upper], wet.at[upper]),
            (field_in, field),
        ))
    ]
    for copy in loads:
        copy.start()
    for copy in loads[:5]:
        copy.wait()
    hot = one_hot_rows(tile_ref[...], offset_ref[...], count_ref[0], cols_n, tile_rows)
    surface = surf[...].reshape(cols_n * tile_rows, LANES)
    saturation = lax.dot_general(
        hot, surface, (((0,), (0,)), ((), ())),
        precision=lax.Precision.HIGHEST, preferred_element_type=jnp.float32,
    )
    patch = lax.broadcasted_iota(jnp.int32, (PATCH_DEV, blocks), 0)
    patch_hot = (patch == patch_ref[...]).astype(jnp.float32)
    patch_out[...] = jnp.dot(
        patch_hot, saturation, precision=lax.Precision.HIGHEST, preferred_element_type=jnp.float32
    )
    used = (lax.broadcasted_iota(jnp.int32, (blocks, LANES), 0) < count_ref[0]).astype(jnp.float32)
    wet_bottom = wet[depth - 1]
    wet[depth - 1] = wet_bottom + capillary * (saturation - used * wet_bottom)
    stores = [
        pltpu.make_async_copy(wet.at[depth - 1], moist_out.at[depth - 1], sem.at[0]),
        pltpu.make_async_copy(wet.at[upper], moist_out.at[upper], sem.at[1]),
        pltpu.make_async_copy(field, head_out, sem.at[2]),
    ]
    stores[0].start()
    for load, store in zip(loads[5:], stores[1:]):
        load.wait()
        store.start()
    for store in stores:
        store.wait()


def local(rows_n, cols_n, moisture, diffusivity, rain, head, conductivity, tile_ids, offsets, patch_ids, counts):
    blocks, depth, _ = moisture.shape
    nz, tile_rows, _ = head.shape
    moisture = jnp.transpose(moisture, (1, 0, 2))
    diffusivity = jnp.transpose(diffusivity, (1, 0, 2))
    tile_ids, offsets, patch_ids = (x.reshape(1, blocks) for x in (tile_ids, offsets, patch_ids))
    f32 = jnp.float32
    per = LANES // SLOT
    groups = pl.cdiv(nz, per)
    ring = (tile_rows + 2 * HALO, 2 * LANES)
    hbm = pl.BlockSpec(memory_space=pltpu.HBM)
    vmem = pl.BlockSpec(memory_space=pltpu.VMEM)
    smem = pl.BlockSpec(memory_space=pltpu.SMEM)
    dma = pltpu.SemaphoreType.DMA
    rech = 3 * cols_n - 1
    field, wet, surf = pl.pallas_call(
        functools.partial(flow_kernel, (rows_n, cols_n, nz, tile_rows)),
        name="flow",
        out_shape=(
            jax.ShapeDtypeStruct((nz, tile_rows, LANES), f32),
            jax.ShapeDtypeStruct((depth, blocks, LANES), f32),
            jax.ShapeDtypeStruct((cols_n, tile_rows, LANES), f32),
        ),
        in_specs=[hbm] * 7 + [smem],
        out_specs=(hbm,) * 3,
        scratch_shapes=[
            pltpu.VMEM((nz, ring[0], LANES), f32),
            pltpu.VMEM((nz, ring[0], LANES), f32),
            pltpu.VMEM((2, ring[0], LANES), f32),
            pltpu.VMEM((nz + 2 * PAD,) + ring, f32),
            pltpu.VMEM((nz + 2 * PAD,) + ring, f32),
            pltpu.VMEM((nz + 2 * PAD,) + ring, f32),
            pltpu.VMEM((nz + 2 * PAD, tile_rows, LANES), f32),
            pltpu.VMEM((nz + 2 * PAD,) + ring, f32),
            pltpu.VMEM((nz + 2 * PAD,) + ring, f32),
            pltpu.VMEM((nz + 2 * PAD,) + ring, f32),
            pltpu.VMEM((nz + 2 * PAD,) + ring, f32),
            pltpu.VMEM((nz + 2 * PAD,) + ring, f32),
            pltpu.VMEM((nz + 2 * PAD,) + ring, f32),
            pltpu.VMEM((SWEEPS + 3,) + ring, f32),
            pltpu.VMEM((SWEEPS + 3,) + ring, f32),
            pltpu.VMEM((2, groups, tile_rows, LANES), f32),
            pltpu.VMEM((2, groups, ring[0], LANES), f32),
            pltpu.VMEM((2, groups, ring[0], LANES), f32),
            pltpu.VMEM((depth, blocks, LANES), f32),
            pltpu.VMEM((depth, blocks, LANES), f32),
            pltpu.VMEM((depth, blocks, LANES), f32),
            pltpu.VMEM((blocks, LANES), f32),
            pltpu.VMEM((1, blocks), jnp.int32),
            pltpu.VMEM((1, blocks), jnp.int32),
            pltpu.VMEM((3, cols_n, cols_n, tile_rows, LANES), f32),
            pltpu.VMEM((cols_n, tile_rows, LANES), f32),
            dma((7,)), dma((3,)), dma((4, nz // CHUNK)), dma((4, nz // CHUNK)), dma((6,)), dma((6,)),
            dma((rech,)), dma((rech,)), dma((cols_n,)), dma((cols_n,)),
        ],
        compiler_params=pltpu.CompilerParams(
            collective_id=0, has_side_effects=True, vmem_limit_bytes=63 * 1024 * 1024
        ),
    )(moisture, diffusivity, rain, head, conductivity, tile_ids, offsets, counts)
    head_out, moist_out, patch_sums = pl.pallas_call(
        functools.partial(exchange_kernel, tile_rows, cols_n),
        name="exchange",
        out_shape=(
            jax.ShapeDtypeStruct((nz, tile_rows, LANES), f32),
            jax.ShapeDtypeStruct((depth, blocks, LANES), f32),
            jax.ShapeDtypeStruct((PATCH_DEV, LANES), f32),
        ),
        in_specs=[hbm] * 6 + [smem],
        out_specs=(hbm, hbm, vmem),
        scratch_shapes=[
            pltpu.VMEM((nz, tile_rows, LANES), f32),
            pltpu.VMEM((depth, blocks, LANES), f32),
            pltpu.VMEM((cols_n, tile_rows, LANES), f32),
            pltpu.VMEM((1, blocks), jnp.int32),
            pltpu.VMEM((1, blocks), jnp.int32),
            pltpu.VMEM((1, blocks), jnp.int32),
            dma((7,)),
        ],
        compiler_params=pltpu.CompilerParams(vmem_limit_bytes=63 * 1024 * 1024),
    )(field, wet, surf, tile_ids, offsets, patch_ids, counts)
    return head_out, jnp.transpose(moist_out, (1, 0, 2)), patch_sums


def solution(mesh):
    placed = (
        P(("gx", "gy"), None, None),
        P(("gx", "gy"), None, None),
        P(("gx", "gy"), None),
        P(None, "gx", "gy"),
        P(None, "gx", "gy"),
        P(("gx", "gy")),
        P(("gx", "gy")),
        P(("gx", "gy")),
        P(("gx", "gy")),
    )
    return jax.shard_map(
        functools.partial(local, mesh.shape["gx"], mesh.shape["gy"]),
        mesh=mesh,
        in_specs=placed,
        out_specs=(P(None, "gx", "gy"), P(("gx", "gy"), None, None), P(("gx", "gy"), None)),
        check_vma=False,
    )
```

```python
import functools

import jax
import jax.numpy as jnp
from jax import lax
from jax.experimental import pallas as pl
from jax.experimental.pallas import tpu as pltpu
from jax.sharding import PartitionSpec as P

PATCH_DEV = 8
SWEEPS = 6
HALO = 8
CHUNK = 10
PAD = CHUNK + 2
SLOT = 2 * HALO
LANES = 128
MESH = pl.DeviceIdType.MESH

flow_rate = 0.15
capillary = 0.5


def one_hot_rows(tile, offset, used_count, tile_count, tile_rows):
    blocks = tile.shape[1]
    block = lax.broadcasted_iota(jnp.int32, (1, blocks), 1)
    target = jnp.where(block < used_count, tile * tile_rows + offset, -1)
    slot = lax.broadcasted_iota(jnp.int32, (tile_count * tile_rows, blocks), 0)
    return (slot == target).astype(jnp.float32)


def flow_kernel(
    sizes,
    moist_in, diff_in, rain_in, head_in, cond_in, tile_in, offset_in, count_ref,
    field_out, wet_out, surf_out,
    h_land, k_land, spread, h, h2, k, field, w_d, w_e, w_w, w_s, w_n, w_v, delta, delta2, packed, land_l, land_r, moist, diff, ratio, rain,
    tile_ref, offset_ref, recharge, surf,
    local_sem, out_sem, row_send, row_recv, pack_send, pack_recv, rech_send, rech_recv,
    surf_send, surf_recv,
):
    rows_n, cols_n, nz, tile_rows = sizes
    gx, gy = lax.axis_index("gx"), lax.axis_index("gy")
    has_below, has_above = gx < rows_n - 1, gx > 0
    has_right, has_left = gy < cols_n - 1, gy > 0
    depth = moist.shape[0]
    groups = packed.shape[1]
    ring_rows, ring_cols = h.shape[1], h.shape[2]
    below = pl.ds(tile_rows, HALO)
    above = pl.ds(tile_rows + HALO, HALO)
    first = pl.ds(0, HALO)
    last = pl.ds(tile_rows - HALO, HALO)
    whole = pl.ds(0, tile_rows)
    layers = pl.ds(PAD, nz)
    chunks = nz // CHUNK

    local = [
        pltpu.make_async_copy(src, dst, local_sem.at[i])
        for i, (src, dst) in enumerate((
            (head_in, h_land.at[:, whole]),
            (cond_in, k_land.at[:, whole]),
            (moist_in, moist),
            (diff_in, diff),
            (rain_in, rain),
            (tile_in, tile_ref),
            (offset_in, offset_ref),
        ))
    ]
    for copy in local:
        copy.start()

    row_steps = ((0, None, whole, whole), (1, has_below, above, last), (-1, has_above, below, first))
    peers = []
    for dx, exists, _, _ in row_steps:
        for dy in range(cols_n):
            if dx or dy:
                peers.append((dx, exists, lax.rem(gy + dy, cols_n)))

    def when(cond, body):
        if cond is None:
            body()
        else:
            pl.when(cond)(body)

    def both(a, b):
        return b if a is None else jnp.logical_and(a, b)

    empty = jnp.zeros((ring_rows, ring_cols), jnp.float32)
    for z in range(PAD):
        for ref in (h, h2, k, w_d, w_e, w_w, w_s, w_n, w_v):
            ref[z] = empty
        for ref in (h, h2, k):
            ref[PAD + nz + z] = empty

    def clear(rows):
        def body(z, _):
            for ref in (h_land, k_land):
                ref[z, rows] = jnp.zeros((HALO, LANES), jnp.float32)
            return 0
        lax.fori_loop(0, nz, body, 0)
    pl.when(gx == 0)(lambda: clear(above))
    pl.when(gx == rows_n - 1)(lambda: clear(below))

    barrier = pltpu.get_barrier_semaphore()
    for dx, exists, col in peers:
        def greet(dx=dx, col=col):
            pl.semaphore_signal(barrier, inc=1, device_id=(gx + dx, col), device_id_type=MESH)
        when(exists, greet)

    local[0].wait()
    local[1].wait()
    lane = lax.broadcasted_iota(jnp.int32, (1, LANES), 1)

    per = LANES // SLOT
    for g in range(groups):
        for f, src in enumerate((h_land, k_land)):
            total = jnp.zeros((tile_rows, LANES), jnp.float32)
            for s in range(min(per, nz - g * per)):
                edge = pltpu.roll(src[g * per + s, 0:tile_rows], (HALO + SLOT * s) % LANES, 1)
                inside = (lane >= SLOT * s) & (lane < SLOT * (s + 1))
                total = jnp.where(inside, edge, total)
            packed[f, g] = total

    def row_copy(i, f, c):
        dx, _, ring, mine = row_steps[1 + i]
        src, dst = ((head_in, h_land), (cond_in, k_land))[f]
        return pltpu.make_async_remote_copy(
            src_ref=src.at[pl.ds(CHUNK * c, CHUNK), mine],
            dst_ref=dst.at[pl.ds(CHUNK * c, CHUNK), ring],
            send_sem=row_send.at[2 * i + f, c],
            recv_sem=row_recv.at[2 * i + f, c],
            device_id=(gx + dx, gy),
            device_id_type=MESH,
        )

    def each_row(cond_of, c, act):
        for i in range(2):
            def body(i=i):
                for f in (1, 0):
                    act(row_copy(i, f, c))
            pl.when(cond_of[i])(body)
    sends_row, gets_row = (has_below, has_above), (has_above, has_below)

    def start_rows(c, _):
        each_row(sends_row, c, lambda copy: copy.start())
        return 0

    def finish_rows(c, _):
        each_row(sends_row, c, lambda copy: copy.wait_send())
        return 0

    pack_copies = []
    n = 0
    for dx, exists, ring, mine in row_steps:
        source_row = None if dx == 0 else (has_above if dx == 1 else has_below)
        for dy, side, target, source in ((1, land_l, has_right, has_left), (-1, land_r, has_left, has_right)):
            pack_copies.append((both(exists, target), both(source_row, source), pltpu.make_async_remote_copy(
                src_ref=packed.at[:, :, mine],
                dst_ref=side.at[:, :, ring],
                send_sem=pack_send.at[n],
                recv_sem=pack_recv.at[n],
                device_id=(gx + dx, gy + dy),
                device_id_type=MESH,
            )))
            n += 1
    near_rows = 1 + has_below.astype(jnp.int32) + has_above.astype(jnp.int32)
    pl.semaphore_wait(barrier, cols_n * near_rows - 1)
    for exists, _, copy in pack_copies:
        when(exists, copy.start)
    lax.fori_loop(0, chunks, start_rows, 0)

    for copy in local[2:]:
        copy.wait()
    e0 = diff[0]
    inv = 1.0 / (1.0 + e0)
    r0, f0 = e0 * inv, (moist[0] + rain[...]) * inv
    ratio[0] = r0
    moist[0] = f0

    def eliminate(layer, carry):
        upper, r, f = carry
        lower = diff[layer]
        inv = 1.0 / (1.0 + lower + upper - upper * r)
        r, f = lower * inv, (moist[layer] + upper * f) * inv
        ratio[layer] = r
        moist[layer] = f
        return lower, r, f
    lower, _, bottom = lax.fori_loop(1, depth, eliminate, (e0, r0, f0))
    drain = lower * bottom
    hot = one_hot_rows(tile_ref[...], offset_ref[...], count_ref[0], cols_n, tile_rows)
    mine = jnp.dot(hot, drain, precision=lax.Precision.HIGHEST, preferred_element_type=jnp.float32)
    recharge[0, gy] = mine.reshape(cols_n, tile_rows, LANES)

    rech_copies = []
    n = 0
    for i, (dx, exists, _, rows) in enumerate(row_steps):
        source_row = None if dx == 0 else (has_above if dx == 1 else has_below)
        for dy in range(0 if dx else 1, cols_n):
            to = lax.rem(gy + dy, cols_n)
            came = lax.rem(gy + cols_n - dy, cols_n)
            def copy(slot, to=to, dx=dx, i=i, rows=rows, n=n):
                return pltpu.make_async_remote_copy(
                    src_ref=recharge.at[0, gy, :, rows],
                    dst_ref=recharge.at[i, slot, :, rows],
                    send_sem=rech_send.at[n],
                    recv_sem=rech_recv.at[n],
                    device_id=(gx + dx, to),
                    device_id_type=MESH,
                )
            rech_copies.append((exists, source_row, copy(gy), copy(came)))
            n += 1
    for exists, _, out, _ in rech_copies:
        when(exists, out.start)

    def substitute(i, wet):
        layer = depth - 2 - i
        wet = moist[layer] + ratio[layer] * wet
        moist[layer] = wet
        return wet
    lax.fori_loop(0, depth - 1, substitute, bottom)
    wet_copy = pltpu.make_async_copy(moist, wet_out, out_sem.at[0])
    wet_copy.start()

    slabs = ring_rows // 8
    place = lax.broadcasted_iota(jnp.int32, (ring_rows, ring_cols), 0)
    ring_row = slabs * (place % 8) + place // 8
    ring_col = lax.broadcasted_iota(jnp.int32, (ring_rows, ring_cols), 1)
    row_ok = (ring_row < tile_rows) | ((ring_row < tile_rows + HALO) & has_below) | ((ring_row >= tile_rows + HALO) & has_above)
    col_ok = (ring_col < LANES) | ((ring_col < LANES + LANES // 2) & has_right) | ((ring_col >= LANES + LANES // 2) & has_left)
    mask = (row_ok & col_ok).astype(jnp.float32)
    on_grid = mask > 0.0

    for _, source, copy in pack_copies:
        when(source, copy.wait_recv)

    def interleaved(ref, *at):
        return jnp.concatenate([ref[(*at, pl.ds(i, 8, stride=slabs))] for i in range(slabs)], axis=0)

    side_on_grid = on_grid[:, LANES:]
    for g in range(groups):
        for f, dst in enumerate((h, k)):
            comb = jnp.where((lane % SLOT) < HALO, interleaved(land_l, f, g), interleaved(land_r, f, g))
            for s in range(min(per, nz - g * per)):
                side = pltpu.roll(comb, (LANES - HALO - SLOT * s) % LANES, 1)
                dst[PAD + g * per + s, :, LANES:] = jnp.where(side_on_grid, side, 0.0)

    scale = 0.5 * flow_rate
    masked = scale * mask

    def east(x):
        return pltpu.roll(x, ring_cols - 1, 1)

    def west(x):
        return pltpu.roll(x, 1, 1)

    def south(x):
        return jnp.concatenate([x[8:], pltpu.roll(x[:8], 7, 0)], axis=0)

    def north(x):
        return jnp.concatenate([pltpu.roll(x[-8:], 1, 0), x[:-8]], axis=0)

    def weights(z0):
        here = k[PAD + z0]
        up = jnp.where((z0 > 0) & (z0 < nz), scale, 0.0) * (k[PAD + z0 - 1] + here)
        for j in range(CHUNK):
            z = z0 + j
            at = PAD + z
            after = k[at + 1]
            down = jnp.where((z >= 0) & (z < nz - 1), scale, 0.0) * (here + after)
            parts = [masked * (here + turn(here)) for turn in (east, west, south, north)]
            for ref, part in zip((w_e, w_w, w_s, w_n), parts):
                ref[at] = part
            w_v[at + 1] = down
            w_d[at] = 1.0 - ((parts[0] + parts[1]) + (parts[2] + parts[3]) + (up + down))
            here, up = after, down

    def step(src, at, w_at, count):
        before, here = src[at - 1], src[at]
        out = []
        for j in range(count):
            w = w_at + j
            after = src[at + j + 1]
            out.append(
                (w_d[w] * here + w_e[w] * east(here))
                + (w_w[w] * west(here) + w_s[w] * south(here))
                + (w_n[w] * north(here) + (w_v[w] * before + w_v[w + 1] * after))
            )
            before, here = here, after
        return out

    tile_part = tile_rows // slabs

    def put_tile(at, new, add):
        for i in range(slabs):
            rows = pl.ds(i, tile_part, stride=slabs)
            part = new[8 * i : 8 * i + tile_part, 0:LANES]
            field[at, rows] = field[at, rows] + part if add else part

    def sweep(n, z0):
        src, dst = (h, h2) if n % 2 == 0 else (h2, h)
        for j, new in enumerate(step(src, PAD + z0, PAD + z0, CHUNK)):
            if n < SWEEPS - 1:
                dst[PAD + z0 + j] = new
            else:
                put_tile(PAD + z0 + j, new, False)

    def wave(c, _):
        @pl.when(c < chunks)
        def _():
            each_row(gets_row, c, lambda copy: copy.wait_recv())
            for j in range(CHUNK):
                z = CHUNK * c + j
                for src, dst in ((h_land, h), (k_land, k)):
                    dst[PAD + z, :, 0:LANES] = interleaved(src, z)

        weights(CHUNK * c - 1)
        for n in range(SWEEPS):
            sweep(n, CHUNK * c - (n + 1))
        return 0
    lax.fori_loop(0, chunks + 1, wave, 0)

    for _, source, _, arrived in rech_copies:
        when(source, arrived.wait_recv)

    def tile_sum(tile):
        parts = []
        for i, rows in ((0, whole), (1, last), (2, first)):
            total = recharge[i, 0, tile, rows]
            for s in range(1, cols_n):
                total = total + recharge[i, s, tile, rows]
            parts.append(total)
        return jnp.concatenate([parts[0], parts[2], parts[1]], axis=0)
    centre = tile_sum(gy)
    right = tile_sum(jnp.minimum(gy + 1, cols_n - 1))
    left = tile_sum(jnp.maximum(gy - 1, 0))
    side = jnp.where(lane < LANES // 2, right, left)
    for z in range(SWEEPS + 3):
        delta[z] = empty
        delta2[z] = empty
    spread[0] = centre
    spread[1] = side
    start = jnp.concatenate([interleaved(spread, 0), interleaved(spread, 1)], axis=1)
    delta[1] = jnp.where(on_grid, start, 0.0)
    for n in range(SWEEPS):
        src, dst = (delta, delta2) if n % 2 == 0 else (delta2, delta)
        for z, new in enumerate(step(src, 1, PAD, min(n + 2, nz))):
            if n < SWEEPS - 1:
                dst[z + 1] = new
            else:
                put_tile(PAD + z, new, True)

    surf[gy] = field[PAD]
    surf_copies = []
    for dy in range(1, cols_n):
        to = lax.rem(gy + dy, cols_n)
        came = lax.rem(gy + cols_n - dy, cols_n)
        pair = [
            pltpu.make_async_remote_copy(
                src_ref=surf.at[gy],
                dst_ref=surf.at[slot],
                send_sem=surf_send.at[dy - 1],
                recv_sem=surf_recv.at[dy - 1],
                device_id=(gx, to),
                device_id_type=MESH,
            )
            for slot in (gy, came)
        ]
        pair[0].start()
        surf_copies.append(pair)
    field_copy = pltpu.make_async_copy(field.at[layers], field_out, out_sem.at[1])
    field_copy.start()
    for _, arrived in surf_copies:
        arrived.wait_recv()
    surf_copy = pltpu.make_async_copy(surf, surf_out, out_sem.at[2])
    surf_copy.start()

    lax.fori_loop(0, chunks, finish_rows, 0)
    for exists, _, copy in pack_copies:
        when(exists, copy.wait_send)
    for exists, _, out, _ in rech_copies:
        when(exists, out.wait_send)
    for out, _ in surf_copies:
        out.wait_send()
    wet_copy.wait()
    field_copy.wait()
    surf_copy.wait()


def exchange_kernel(
    tile_rows, cols_n,
    field_in, wet_in, surf_in, tile_in, offset_in, patch_in, count_ref,
    head_out, moist_out, patch_out,
    field, wet, surf, tile_ref, offset_ref, patch_ref, sem,
):
    depth, blocks, _ = wet.shape
    upper = pl.ds(0, depth - 1)
    loads = [
        pltpu.make_async_copy(src, dst, sem.at[i])
        for i, (src, dst) in enumerate((
            (tile_in, tile_ref),
            (offset_in, offset_ref),
            (patch_in, patch_ref),
            (surf_in, surf),
            (wet_in.at[depth - 1], wet.at[depth - 1]),
            (wet_in.at[upper], wet.at[upper]),
            (field_in, field),
        ))
    ]
    for copy in loads:
        copy.start()
    for copy in loads[:5]:
        copy.wait()
    hot = one_hot_rows(tile_ref[...], offset_ref[...], count_ref[0], cols_n, tile_rows)
    surface = surf[...].reshape(cols_n * tile_rows, LANES)
    saturation = lax.dot_general(
        hot, surface, (((0,), (0,)), ((), ())),
        precision=lax.Precision.HIGHEST, preferred_element_type=jnp.float32,
    )
    patch = lax.broadcasted_iota(jnp.int32, (PATCH_DEV, blocks), 0)
    patch_hot = (patch == patch_ref[...]).astype(jnp.float32)
    patch_out[...] = jnp.dot(
        patch_hot, saturation, precision=lax.Precision.HIGHEST, preferred_element_type=jnp.float32
    )
    used = (lax.broadcasted_iota(jnp.int32, (blocks, LANES), 0) < count_ref[0]).astype(jnp.float32)
    wet_bottom = wet[depth - 1]
    wet[depth - 1] = wet_bottom + capillary * (saturation - used * wet_bottom)
    stores = [
        pltpu.make_async_copy(wet.at[depth - 1], moist_out.at[depth - 1], sem.at[0]),
        pltpu.make_async_copy(wet.at[upper], moist_out.at[upper], sem.at[1]),
        pltpu.make_async_copy(field, head_out, sem.at[2]),
    ]
    stores[0].start()
    for load, store in zip(loads[5:], stores[1:]):
        load.wait()
        store.start()
    for store in stores:
        store.wait()


def local(rows_n, cols_n, moisture, diffusivity, rain, head, conductivity, tile_ids, offsets, patch_ids, counts):
    blocks, depth, _ = moisture.shape
    nz, tile_rows, _ = head.shape
    moisture = jnp.transpose(moisture, (1, 0, 2))
    diffusivity = jnp.transpose(diffusivity, (1, 0, 2))
    tile_ids, offsets, patch_ids = (x.reshape(1, blocks) for x in (tile_ids, offsets, patch_ids))
    f32 = jnp.float32
    per = LANES // SLOT
    groups = pl.cdiv(nz, per)
    ring = (tile_rows + 2 * HALO, 2 * LANES)
    hbm = pl.BlockSpec(memory_space=pltpu.HBM)
    vmem = pl.BlockSpec(memory_space=pltpu.VMEM)
    smem = pl.BlockSpec(memory_space=pltpu.SMEM)
    dma = pltpu.SemaphoreType.DMA
    rech = 3 * cols_n - 1
    field, wet, surf = pl.pallas_call(
        functools.partial(flow_kernel, (rows_n, cols_n, nz, tile_rows)),
        name="flow",
        out_shape=(
            jax.ShapeDtypeStruct((nz, tile_rows, LANES), f32),
            jax.ShapeDtypeStruct((depth, blocks, LANES), f32),
            jax.ShapeDtypeStruct((cols_n, tile_rows, LANES), f32),
        ),
        in_specs=[hbm] * 7 + [smem],
        out_specs=(hbm,) * 3,
        scratch_shapes=[
            pltpu.VMEM((nz, ring[0], LANES), f32),
            pltpu.VMEM((nz, ring[0], LANES), f32),
            pltpu.VMEM((2, ring[0], LANES), f32),
            pltpu.VMEM((nz + 2 * PAD,) + ring, f32),
            pltpu.VMEM((nz + 2 * PAD,) + ring, f32),
            pltpu.VMEM((nz + 2 * PAD,) + ring, f32),
            pltpu.VMEM((nz + 2 * PAD, tile_rows, LANES), f32),
            pltpu.VMEM((nz + 2 * PAD,) + ring, f32),
            pltpu.VMEM((nz + 2 * PAD,) + ring, f32),
            pltpu.VMEM((nz + 2 * PAD,) + ring, f32),
            pltpu.VMEM((nz + 2 * PAD,) + ring, f32),
            pltpu.VMEM((nz + 2 * PAD,) + ring, f32),
            pltpu.VMEM((nz + 2 * PAD,) + ring, f32),
            pltpu.VMEM((SWEEPS + 3,) + ring, f32),
            pltpu.VMEM((SWEEPS + 3,) + ring, f32),
            pltpu.VMEM((2, groups, tile_rows, LANES), f32),
            pltpu.VMEM((2, groups, ring[0], LANES), f32),
            pltpu.VMEM((2, groups, ring[0], LANES), f32),
            pltpu.VMEM((depth, blocks, LANES), f32),
            pltpu.VMEM((depth, blocks, LANES), f32),
            pltpu.VMEM((depth, blocks, LANES), f32),
            pltpu.VMEM((blocks, LANES), f32),
            pltpu.VMEM((1, blocks), jnp.int32),
            pltpu.VMEM((1, blocks), jnp.int32),
            pltpu.VMEM((3, cols_n, cols_n, tile_rows, LANES), f32),
            pltpu.VMEM((cols_n, tile_rows, LANES), f32),
            dma((7,)), dma((3,)), dma((4, nz // CHUNK)), dma((4, nz // CHUNK)), dma((6,)), dma((6,)),
            dma((rech,)), dma((rech,)), dma((cols_n,)), dma((cols_n,)),
        ],
        compiler_params=pltpu.CompilerParams(
            collective_id=0, has_side_effects=True, vmem_limit_bytes=63 * 1024 * 1024
        ),
    )(moisture, diffusivity, rain, head, conductivity, tile_ids, offsets, counts)
    head_out, moist_out, patch_sums = pl.pallas_call(
        functools.partial(exchange_kernel, tile_rows, cols_n),
        name="exchange",
        out_shape=(
            jax.ShapeDtypeStruct((nz, tile_rows, LANES), f32),
            jax.ShapeDtypeStruct((depth, blocks, LANES), f32),
            jax.ShapeDtypeStruct((PATCH_DEV, LANES), f32),
        ),
        in_specs=[hbm] * 6 + [smem],
        out_specs=(hbm, hbm, vmem),
        scratch_shapes=[
            pltpu.VMEM((nz, tile_rows, LANES), f32),
            pltpu.VMEM((depth, blocks, LANES), f32),
            pltpu.VMEM((cols_n, tile_rows, LANES), f32),
            pltpu.VMEM((1, blocks), jnp.int32),
            pltpu.VMEM((1, blocks), jnp.int32),
            pltpu.VMEM((1, blocks), jnp.int32),
            dma((7,)),
        ],
        compiler_params=pltpu.CompilerParams(vmem_limit_bytes=63 * 1024 * 1024),
    )(field, wet, surf, tile_ids, offsets, patch_ids, counts)
    return head_out, jnp.transpose(moist_out, (1, 0, 2)), patch_sums


def solution(mesh):
    placed = (
        P(("gx", "gy"), None, None),
        P(("gx", "gy"), None, None),
        P(("gx", "gy"), None),
        P(None, "gx", "gy"),
        P(None, "gx", "gy"),
        P(("gx", "gy")),
        P(("gx", "gy")),
        P(("gx", "gy")),
        P(("gx", "gy")),
    )
    return jax.shard_map(
        functools.partial(local, mesh.shape["gx"], mesh.shape["gy"]),
        mesh=mesh,
        in_specs=placed,
        out_specs=(P(None, "gx", "gy"), P(("gx", "gy"), None, None), P(("gx", "gy"), None)),
        check_vma=False,
    )
```

```python
import functools

import jax
import jax.numpy as jnp
from jax import lax
from jax.experimental import pallas as pl
from jax.experimental.pallas import tpu as pltpu
from jax.sharding import PartitionSpec as P

PATCH_DEV = 8
SWEEPS = 6
HALO = 8
CHUNK = 10
PAD = CHUNK + 2
SLOT = 2 * HALO
LANES = 128
MESH = pl.DeviceIdType.MESH

flow_rate = 0.15
capillary = 0.5


def one_hot_rows(tile, offset, used_count, tile_count, tile_rows):
    blocks = tile.shape[1]
    block = lax.broadcasted_iota(jnp.int32, (1, blocks), 1)
    target = jnp.where(block < used_count, tile * tile_rows + offset, -1)
    slot = lax.broadcasted_iota(jnp.int32, (tile_count * tile_rows, blocks), 0)
    return (slot == target).astype(jnp.float32)


def flow_kernel(
    sizes,
    moist_in, diff_in, rain_in, head_in, cond_in, tile_in, offset_in, count_ref,
    field_out, wet_out, surf_out,
    h_land, k_land, spread, h, h2, k, field, w_d, w_e, w_w, w_s, w_n, w_v, delta, delta2, packed, land_l, land_r, moist, diff, ratio, rain,
    tile_ref, offset_ref, recharge, surf,
    local_sem, out_sem, row_send, row_recv, pack_send, pack_recv, rech_send, rech_recv,
    surf_send, surf_recv,
):
    rows_n, cols_n, nz, tile_rows = sizes
    gx, gy = lax.axis_index("gx"), lax.axis_index("gy")
    has_below, has_above = gx < rows_n - 1, gx > 0
    has_right, has_left = gy < cols_n - 1, gy > 0
    depth = moist.shape[0]
    groups = packed.shape[1]
    ring_rows, ring_cols = h.shape[1], h.shape[2]
    below = pl.ds(tile_rows, HALO)
    above = pl.ds(tile_rows + HALO, HALO)
    first = pl.ds(0, HALO)
    last = pl.ds(tile_rows - HALO, HALO)
    whole = pl.ds(0, tile_rows)
    layers = pl.ds(PAD, nz)
    chunks = nz // CHUNK

    local = [
        pltpu.make_async_copy(src, dst, local_sem.at[i])
        for i, (src, dst) in enumerate((
            (head_in, h_land.at[:, whole]),
            (cond_in, k_land.at[:, whole]),
            (moist_in, moist),
            (diff_in, diff),
            (rain_in, rain),
            (tile_in, tile_ref),
            (offset_in, offset_ref),
        ))
    ]
    for copy in local:
        copy.start()

    row_steps = ((0, None, whole, whole), (1, has_below, above, last), (-1, has_above, below, first))
    peers = []
    for dx, exists, _, _ in row_steps:
        for dy in range(cols_n):
            if dx or dy:
                peers.append((dx, exists, lax.rem(gy + dy, cols_n)))

    def when(cond, body):
        if cond is None:
            body()
        else:
            pl.when(cond)(body)

    def both(a, b):
        return b if a is None else jnp.logical_and(a, b)

    empty = jnp.zeros((ring_rows, ring_cols), jnp.float32)
    for z in range(PAD):
        for ref in (h, h2, k, w_d, w_e, w_w, w_s, w_n, w_v):
            ref[z] = empty
        for ref in (h, h2, k):
            ref[PAD + nz + z] = empty

    def clear(rows):
        def body(z, _):
            for ref in (h_land, k_land):
                ref[z, rows] = jnp.zeros((HALO, LANES), jnp.float32)
            return 0
        lax.fori_loop(0, nz, body, 0)
    pl.when(gx == 0)(lambda: clear(above))
    pl.when(gx == rows_n - 1)(lambda: clear(below))

    barrier = pltpu.get_barrier_semaphore()
    for dx, exists, col in peers:
        def greet(dx=dx, col=col):
            pl.semaphore_signal(barrier, inc=1, device_id=(gx + dx, col), device_id_type=MESH)
        when(exists, greet)

    local[0].wait()
    local[1].wait()
    lane = lax.broadcasted_iota(jnp.int32, (1, LANES), 1)

    per = LANES // SLOT
    for g in range(groups):
        for f, src in enumerate((h_land, k_land)):
            total = jnp.zeros((tile_rows, LANES), jnp.float32)
            for s in range(min(per, nz - g * per)):
                edge = pltpu.roll(src[g * per + s, 0:tile_rows], (HALO + SLOT * s) % LANES, 1)
                inside = (lane >= SLOT * s) & (lane < SLOT * (s + 1))
                total = jnp.where(inside, edge, total)
            packed[f, g] = total

    def row_copy(i, f, c):
        dx, _, ring, mine = row_steps[1 + i]
        src, dst = ((head_in, h_land), (cond_in, k_land))[f]
        return pltpu.make_async_remote_copy(
            src_ref=src.at[pl.ds(CHUNK * c, CHUNK), mine],
            dst_ref=dst.at[pl.ds(CHUNK * c, CHUNK), ring],
            send_sem=row_send.at[2 * i + f, c],
            recv_sem=row_recv.at[2 * i + f, c],
            device_id=(gx + dx, gy),
            device_id_type=MESH,
        )

    def each_row(cond_of, c, act):
        for i in range(2):
            def body(i=i):
                for f in (1, 0):
                    act(row_copy(i, f, c))
            pl.when(cond_of[i])(body)
    sends_row, gets_row = (has_below, has_above), (has_above, has_below)

    def start_rows(c, _):
        each_row(sends_row, c, lambda copy: copy.start())
        return 0

    def finish_rows(c, _):
        each_row(sends_row, c, lambda copy: copy.wait_send())
        return 0

    pack_copies = []
    n = 0
    for dx, exists, ring, mine in row_steps:
        source_row = None if dx == 0 else (has_above if dx == 1 else has_below)
        for dy, side, target, source in ((1, land_l, has_right, has_left), (-1, land_r, has_left, has_right)):
            pack_copies.append((both(exists, target), both(source_row, source), pltpu.make_async_remote_copy(
                src_ref=packed.at[:, :, mine],
                dst_ref=side.at[:, :, ring],
                send_sem=pack_send.at[n],
                recv_sem=pack_recv.at[n],
                device_id=(gx + dx, gy + dy),
                device_id_type=MESH,
            )))
            n += 1
    near_rows = 1 + has_below.astype(jnp.int32) + has_above.astype(jnp.int32)
    pl.semaphore_wait(barrier, cols_n * near_rows - 1)
    for exists, _, copy in pack_copies:
        when(exists, copy.start)
    lax.fori_loop(0, chunks, start_rows, 0)

    for copy in local[2:]:
        copy.wait()
    e0 = diff[0]
    inv = 1.0 / (1.0 + e0)
    r0, f0 = e0 * inv, (moist[0] + rain[...]) * inv
    ratio[0] = r0
    moist[0] = f0

    def eliminate(layer, carry):
        upper, r, f = carry
        lower = diff[layer]
        inv = 1.0 / (1.0 + lower + upper - upper * r)
        r, f = lower * inv, (moist[layer] + upper * f) * inv
        ratio[layer] = r
        moist[layer] = f
        return lower, r, f
    lower, _, bottom = lax.fori_loop(1, depth, eliminate, (e0, r0, f0), unroll=True)
    drain = lower * bottom
    hot = one_hot_rows(tile_ref[...], offset_ref[...], count_ref[0], cols_n, tile_rows)
    mine = jnp.dot(hot, drain, precision=lax.Precision.HIGHEST, preferred_element_type=jnp.float32)
    recharge[0, gy] = mine.reshape(cols_n, tile_rows, LANES)

    rech_copies = []
    n = 0
    for i, (dx, exists, _, rows) in enumerate(row_steps):
        source_row = None if dx == 0 else (has_above if dx == 1 else has_below)
        for dy in range(0 if dx else 1, cols_n):
            to = lax.rem(gy + dy, cols_n)
            came = lax.rem(gy + cols_n - dy, cols_n)
            def copy(slot, to=to, dx=dx, i=i, rows=rows, n=n):
                return pltpu.make_async_remote_copy(
                    src_ref=recharge.at[0, gy, :, rows],
                    dst_ref=recharge.at[i, slot, :, rows],
                    send_sem=rech_send.at[n],
                    recv_sem=rech_recv.at[n],
                    device_id=(gx + dx, to),
                    device_id_type=MESH,
                )
            rech_copies.append((exists, source_row, copy(gy), copy(came)))
            n += 1
    for exists, _, out, _ in rech_copies:
        when(exists, out.start)

    def substitute(i, wet):
        layer = depth - 2 - i
        wet = moist[layer] + ratio[layer] * wet
        moist[layer] = wet
        return wet
    lax.fori_loop(0, depth - 1, substitute, bottom, unroll=True)
    wet_copy = pltpu.make_async_copy(moist, wet_out, out_sem.at[0])
    wet_copy.start()

    slabs = ring_rows // 8
    place = lax.broadcasted_iota(jnp.int32, (ring_rows, ring_cols), 0)
    ring_row = slabs * (place % 8) + place // 8
    ring_col = lax.broadcasted_iota(jnp.int32, (ring_rows, ring_cols), 1)
    row_ok = (ring_row < tile_rows) | ((ring_row < tile_rows + HALO) & has_below) | ((ring_row >= tile_rows + HALO) & has_above)
    col_ok = (ring_col < LANES) | ((ring_col < LANES + LANES // 2) & has_right) | ((ring_col >= LANES + LANES // 2) & has_left)
    mask = (row_ok & col_ok).astype(jnp.float32)
    on_grid = mask > 0.0

    for _, source, copy in pack_copies:
        when(source, copy.wait_recv)

    def interleaved(ref, *at):
        return jnp.concatenate([ref[(*at, pl.ds(i, 8, stride=slabs))] for i in range(slabs)], axis=0)

    side_on_grid = on_grid[:, LANES:]
    for g in range(groups):
        for f, dst in enumerate((h, k)):
            comb = jnp.where((lane % SLOT) < HALO, interleaved(land_l, f, g), interleaved(land_r, f, g))
            for s in range(min(per, nz - g * per)):
                side = pltpu.roll(comb, (LANES - HALO - SLOT * s) % LANES, 1)
                dst[PAD + g * per + s, :, LANES:] = jnp.where(side_on_grid, side, 0.0)

    scale = 0.5 * flow_rate
    masked = scale * mask

    def east(x):
        return pltpu.roll(x, ring_cols - 1, 1)

    def west(x):
        return pltpu.roll(x, 1, 1)

    def south(x):
        return jnp.concatenate([x[8:], pltpu.roll(x[:8], 7, 0)], axis=0)

    def north(x):
        return jnp.concatenate([pltpu.roll(x[-8:], 1, 0), x[:-8]], axis=0)

    def weights(z0):
        here = k[PAD + z0]
        up = jnp.where((z0 > 0) & (z0 < nz), scale, 0.0) * (k[PAD + z0 - 1] + here)
        for j in range(CHUNK):
            z = z0 + j
            at = PAD + z
            after = k[at + 1]
            down = jnp.where((z >= 0) & (z < nz - 1), scale, 0.0) * (here + after)
            parts = [masked * (here + turn(here)) for turn in (east, west, south, north)]
            for ref, part in zip((w_e, w_w, w_s, w_n), parts):
                ref[at] = part
            w_v[at + 1] = down
            w_d[at] = 1.0 - ((parts[0] + parts[1]) + (parts[2] + parts[3]) + (up + down))
            here, up = after, down

    def step(src, at, w_at, count):
        before, here = src[at - 1], src[at]
        out = []
        for j in range(count):
            w = w_at + j
            after = src[at + j + 1]
            out.append(
                (w_d[w] * here + w_e[w] * east(here))
                + (w_w[w] * west(here) + w_s[w] * south(here))
                + (w_n[w] * north(here) + (w_v[w] * before + w_v[w + 1] * after))
            )
            before, here = here, after
        return out

    tile_part = tile_rows // slabs

    def put_tile(at, new, add):
        for i in range(slabs):
            rows = pl.ds(i, tile_part, stride=slabs)
            part = new[8 * i : 8 * i + tile_part, 0:LANES]
            field[at, rows] = field[at, rows] + part if add else part

    def sweep(n, z0):
        src, dst = (h, h2) if n % 2 == 0 else (h2, h)
        for j, new in enumerate(step(src, PAD + z0, PAD + z0, CHUNK)):
            if n < SWEEPS - 1:
                dst[PAD + z0 + j] = new
            else:
                put_tile(PAD + z0 + j, new, False)

    surf_copies = []
    for dy in range(1, cols_n):
        to = lax.rem(gy + dy, cols_n)
        came = lax.rem(gy + cols_n - dy, cols_n)
        pair = [
            pltpu.make_async_remote_copy(
                src_ref=surf.at[gy],
                dst_ref=surf.at[slot],
                send_sem=surf_send.at[dy - 1],
                recv_sem=surf_recv.at[dy - 1],
                device_id=(gx, to),
                device_id_type=MESH,
            )
            for slot in (gy, came)
        ]
        surf_copies.append(pair)

    def finish_top():
        for _, source, _, arrived in rech_copies:
            when(source, arrived.wait_recv)

        def tile_sum(tile):
            parts = []
            for i, rows in ((0, whole), (1, last), (2, first)):
                total = recharge[i, 0, tile, rows]
                for s in range(1, cols_n):
                    total = total + recharge[i, s, tile, rows]
                parts.append(total)
            return jnp.concatenate([parts[0], parts[2], parts[1]], axis=0)
        centre = tile_sum(gy)
        right = tile_sum(jnp.minimum(gy + 1, cols_n - 1))
        left = tile_sum(jnp.maximum(gy - 1, 0))
        side = jnp.where(lane < LANES // 2, right, left)
        for z in range(SWEEPS + 3):
            delta[z] = empty
            delta2[z] = empty
        spread[0] = centre
        spread[1] = side
        start = jnp.concatenate([interleaved(spread, 0), interleaved(spread, 1)], axis=1)
        delta[1] = jnp.where(on_grid, start, 0.0)
        for n in range(SWEEPS):
            src, dst = (delta, delta2) if n % 2 == 0 else (delta2, delta)
            for z, new in enumerate(step(src, 1, PAD, min(n + 2, nz))):
                if n < SWEEPS - 1:
                    dst[z + 1] = new
                else:
                    put_tile(PAD + z, new, True)
        surf[gy] = field[PAD]
        for out, _ in surf_copies:
            out.start()

    def wave(c, _):
        @pl.when(c < chunks)
        def _():
            each_row(gets_row, c, lambda copy: copy.wait_recv())
            for j in range(CHUNK):
                z = CHUNK * c + j
                for src, dst in ((h_land, h), (k_land, k)):
                    dst[PAD + z, :, 0:LANES] = interleaved(src, z)

        weights(CHUNK * c - 1)
        for n in range(SWEEPS):
            sweep(n, CHUNK * c - (n + 1))
        pl.when(c == 1)(finish_top)
        return 0
    lax.fori_loop(0, chunks + 1, wave, 0)

    field_copy = pltpu.make_async_copy(field.at[layers], field_out, out_sem.at[1])
    field_copy.start()
    for _, arrived in surf_copies:
        arrived.wait_recv()
    surf_copy = pltpu.make_async_copy(surf, surf_out, out_sem.at[2])
    surf_copy.start()

    lax.fori_loop(0, chunks, finish_rows, 0)
    for exists, _, copy in pack_copies:
        when(exists, copy.wait_send)
    for exists, _, out, _ in rech_copies:
        when(exists, out.wait_send)
    for out, _ in surf_copies:
        out.wait_send()
    wet_copy.wait()
    field_copy.wait()
    surf_copy.wait()


def exchange_kernel(
    tile_rows, cols_n,
    field_in, wet_in, surf_in, tile_in, offset_in, patch_in, count_ref,
    head_out, moist_out, patch_out,
    field, wet, surf, tile_ref, offset_ref, patch_ref, sem,
):
    depth, blocks, _ = wet.shape
    upper = pl.ds(0, depth - 1)
    loads = [
        pltpu.make_async_copy(src, dst, sem.at[i])
        for i, (src, dst) in enumerate((
            (tile_in, tile_ref),
            (offset_in, offset_ref),
            (patch_in, patch_ref),
            (surf_in, surf),
            (wet_in.at[depth - 1], wet.at[depth - 1]),
            (wet_in.at[upper], wet.at[upper]),
            (field_in, field),
        ))
    ]
    for copy in loads:
        copy.start()
    for copy in loads[:5]:
        copy.wait()
    hot = one_hot_rows(tile_ref[...], offset_ref[...], count_ref[0], cols_n, tile_rows)
    surface = surf[...].reshape(cols_n * tile_rows, LANES)
    saturation = lax.dot_general(
        hot, surface, (((0,), (0,)), ((), ())),
        precision=lax.Precision.HIGHEST, preferred_element_type=jnp.float32,
    )
    patch = lax.broadcasted_iota(jnp.int32, (PATCH_DEV, blocks), 0)
    patch_hot = (patch == patch_ref[...]).astype(jnp.float32)
    patch_out[...] = jnp.dot(
        patch_hot, saturation, precision=lax.Precision.HIGHEST, preferred_element_type=jnp.float32
    )
    used = (lax.broadcasted_iota(jnp.int32, (blocks, LANES), 0) < count_ref[0]).astype(jnp.float32)
    wet_bottom = wet[depth - 1]
    wet[depth - 1] = wet_bottom + capillary * (saturation - used * wet_bottom)
    stores = [
        pltpu.make_async_copy(wet.at[depth - 1], moist_out.at[depth - 1], sem.at[0]),
        pltpu.make_async_copy(wet.at[upper], moist_out.at[upper], sem.at[1]),
        pltpu.make_async_copy(field, head_out, sem.at[2]),
    ]
    stores[0].start()
    for load, store in zip(loads[5:], stores[1:]):
        load.wait()
        store.start()
    for store in stores:
        store.wait()


def local(rows_n, cols_n, moisture, diffusivity, rain, head, conductivity, tile_ids, offsets, patch_ids, counts):
    blocks, depth, _ = moisture.shape
    nz, tile_rows, _ = head.shape
    moisture = jnp.transpose(moisture, (1, 0, 2))
    diffusivity = jnp.transpose(diffusivity, (1, 0, 2))
    tile_ids, offsets, patch_ids = (x.reshape(1, blocks) for x in (tile_ids, offsets, patch_ids))
    f32 = jnp.float32
    per = LANES // SLOT
    groups = pl.cdiv(nz, per)
    ring = (tile_rows + 2 * HALO, 2 * LANES)
    hbm = pl.BlockSpec(memory_space=pltpu.HBM)
    vmem = pl.BlockSpec(memory_space=pltpu.VMEM)
    smem = pl.BlockSpec(memory_space=pltpu.SMEM)
    dma = pltpu.SemaphoreType.DMA
    rech = 3 * cols_n - 1
    field, wet, surf = pl.pallas_call(
        functools.partial(flow_kernel, (rows_n, cols_n, nz, tile_rows)),
        name="flow",
        out_shape=(
            jax.ShapeDtypeStruct((nz, tile_rows, LANES), f32),
            jax.ShapeDtypeStruct((depth, blocks, LANES), f32),
            jax.ShapeDtypeStruct((cols_n, tile_rows, LANES), f32),
        ),
        in_specs=[hbm] * 7 + [smem],
        out_specs=(hbm,) * 3,
        scratch_shapes=[
            pltpu.VMEM((nz, ring[0], LANES), f32),
            pltpu.VMEM((nz, ring[0], LANES), f32),
            pltpu.VMEM((2, ring[0], LANES), f32),
            pltpu.VMEM((nz + 2 * PAD,) + ring, f32),
            pltpu.VMEM((nz + 2 * PAD,) + ring, f32),
            pltpu.VMEM((nz + 2 * PAD,) + ring, f32),
            pltpu.VMEM((nz + 2 * PAD, tile_rows, LANES), f32),
            pltpu.VMEM((nz + 2 * PAD,) + ring, f32),
            pltpu.VMEM((nz + 2 * PAD,) + ring, f32),
            pltpu.VMEM((nz + 2 * PAD,) + ring, f32),
            pltpu.VMEM((nz + 2 * PAD,) + ring, f32),
            pltpu.VMEM((nz + 2 * PAD,) + ring, f32),
            pltpu.VMEM((nz + 2 * PAD,) + ring, f32),
            pltpu.VMEM((SWEEPS + 3,) + ring, f32),
            pltpu.VMEM((SWEEPS + 3,) + ring, f32),
            pltpu.VMEM((2, groups, tile_rows, LANES), f32),
            pltpu.VMEM((2, groups, ring[0], LANES), f32),
            pltpu.VMEM((2, groups, ring[0], LANES), f32),
            pltpu.VMEM((depth, blocks, LANES), f32),
            pltpu.VMEM((depth, blocks, LANES), f32),
            pltpu.VMEM((depth, blocks, LANES), f32),
            pltpu.VMEM((blocks, LANES), f32),
            pltpu.VMEM((1, blocks), jnp.int32),
            pltpu.VMEM((1, blocks), jnp.int32),
            pltpu.VMEM((3, cols_n, cols_n, tile_rows, LANES), f32),
            pltpu.VMEM((cols_n, tile_rows, LANES), f32),
            dma((7,)), dma((3,)), dma((4, nz // CHUNK)), dma((4, nz // CHUNK)), dma((6,)), dma((6,)),
            dma((rech,)), dma((rech,)), dma((cols_n,)), dma((cols_n,)),
        ],
        compiler_params=pltpu.CompilerParams(
            collective_id=0, has_side_effects=True, vmem_limit_bytes=63 * 1024 * 1024
        ),
    )(moisture, diffusivity, rain, head, conductivity, tile_ids, offsets, counts)
    head_out, moist_out, patch_sums = pl.pallas_call(
        functools.partial(exchange_kernel, tile_rows, cols_n),
        name="exchange",
        out_shape=(
            jax.ShapeDtypeStruct((nz, tile_rows, LANES), f32),
            jax.ShapeDtypeStruct((depth, blocks, LANES), f32),
            jax.ShapeDtypeStruct((PATCH_DEV, LANES), f32),
        ),
        in_specs=[hbm] * 6 + [smem],
        out_specs=(hbm, hbm, vmem),
        scratch_shapes=[
            pltpu.VMEM((nz, tile_rows, LANES), f32),
            pltpu.VMEM((depth, blocks, LANES), f32),
            pltpu.VMEM((cols_n, tile_rows, LANES), f32),
            pltpu.VMEM((1, blocks), jnp.int32),
            pltpu.VMEM((1, blocks), jnp.int32),
            pltpu.VMEM((1, blocks), jnp.int32),
            dma((7,)),
        ],
        compiler_params=pltpu.CompilerParams(vmem_limit_bytes=63 * 1024 * 1024),
    )(field, wet, surf, tile_ids, offsets, patch_ids, counts)
    return head_out, jnp.transpose(moist_out, (1, 0, 2)), patch_sums


def solution(mesh):
    placed = (
        P(("gx", "gy"), None, None),
        P(("gx", "gy"), None, None),
        P(("gx", "gy"), None),
        P(None, "gx", "gy"),
        P(None, "gx", "gy"),
        P(("gx", "gy")),
        P(("gx", "gy")),
        P(("gx", "gy")),
        P(("gx", "gy")),
    )
    return jax.shard_map(
        functools.partial(local, mesh.shape["gx"], mesh.shape["gy"]),
        mesh=mesh,
        in_specs=placed,
        out_specs=(P(None, "gx", "gy"), P(("gx", "gy"), None, None), P(("gx", "gy"), None)),
        check_vma=False,
    )
```

```python
import functools

import jax
import jax.numpy as jnp
from jax import lax
from jax.experimental import pallas as pl
from jax.experimental.pallas import tpu as pltpu
from jax.sharding import PartitionSpec as P

PATCH_DEV = 8
SWEEPS = 6
HALO = 8
CHUNK = 10
PAD = CHUNK + 2
SLOT = 2 * HALO
LANES = 128
MESH = pl.DeviceIdType.MESH

flow_rate = 0.15
capillary = 0.5


def one_hot_rows(tile, offset, used_count, tile_count, tile_rows):
    blocks = tile.shape[1]
    block = lax.broadcasted_iota(jnp.int32, (1, blocks), 1)
    target = jnp.where(block < used_count, tile * tile_rows + offset, -1)
    slot = lax.broadcasted_iota(jnp.int32, (tile_count * tile_rows, blocks), 0)
    return (slot == target).astype(jnp.float32)


def flow_kernel(
    sizes,
    moist_in, diff_in, rain_in, head_in, cond_in, tile_in, offset_in, count_ref,
    field_out, wet_out, surf_out,
    h_land, k_land, spread, h, h2, k, field, w_d, w_e, w_w, w_s, w_n, w_v, delta, delta2, packed, land_l, land_r, moist, diff, ratio, rain,
    tile_ref, offset_ref, recharge, surf,
    local_sem, out_sem, field_sem, row_send, row_recv, pack_send, pack_recv, rech_send, rech_recv,
    surf_send, surf_recv,
):
    rows_n, cols_n, nz, tile_rows = sizes
    gx, gy = lax.axis_index("gx"), lax.axis_index("gy")
    has_below, has_above = gx < rows_n - 1, gx > 0
    has_right, has_left = gy < cols_n - 1, gy > 0
    depth = moist.shape[0]
    groups = packed.shape[1]
    ring_rows, ring_cols = h.shape[1], h.shape[2]
    below = pl.ds(tile_rows, HALO)
    above = pl.ds(tile_rows + HALO, HALO)
    first = pl.ds(0, HALO)
    last = pl.ds(tile_rows - HALO, HALO)
    whole = pl.ds(0, tile_rows)
    layers = pl.ds(PAD, nz)
    chunks = nz // CHUNK

    local = [
        pltpu.make_async_copy(src, dst, local_sem.at[i])
        for i, (src, dst) in enumerate((
            (head_in, h_land.at[:, whole]),
            (cond_in, k_land.at[:, whole]),
            (moist_in, moist),
            (diff_in, diff),
            (rain_in, rain),
            (tile_in, tile_ref),
            (offset_in, offset_ref),
        ))
    ]
    for copy in local:
        copy.start()

    row_steps = ((0, None, whole, whole), (1, has_below, above, last), (-1, has_above, below, first))
    peers = []
    for dx, exists, _, _ in row_steps:
        for dy in range(cols_n):
            if dx or dy:
                peers.append((dx, exists, lax.rem(gy + dy, cols_n)))

    def when(cond, body):
        if cond is None:
            body()
        else:
            pl.when(cond)(body)

    def both(a, b):
        return b if a is None else jnp.logical_and(a, b)

    empty = jnp.zeros((ring_rows, ring_cols), jnp.float32)
    for z in range(PAD):
        for ref in (h, h2, k, w_d, w_e, w_w, w_s, w_n, w_v):
            ref[z] = empty
        for ref in (h, h2, k):
            ref[PAD + nz + z] = empty

    def clear(rows):
        def body(z, _):
            for ref in (h_land, k_land):
                ref[z, rows] = jnp.zeros((HALO, LANES), jnp.float32)
            return 0
        lax.fori_loop(0, nz, body, 0)
    pl.when(gx == 0)(lambda: clear(above))
    pl.when(gx == rows_n - 1)(lambda: clear(below))

    barrier = pltpu.get_barrier_semaphore()
    for dx, exists, col in peers:
        def greet(dx=dx, col=col):
            pl.semaphore_signal(barrier, inc=1, device_id=(gx + dx, col), device_id_type=MESH)
        when(exists, greet)

    local[0].wait()
    local[1].wait()
    lane = lax.broadcasted_iota(jnp.int32, (1, LANES), 1)

    per = LANES // SLOT
    for g in range(groups):
        for f, src in enumerate((h_land, k_land)):
            total = jnp.zeros((tile_rows, LANES), jnp.float32)
            for s in range(min(per, nz - g * per)):
                edge = pltpu.roll(src[g * per + s, 0:tile_rows], (HALO + SLOT * s) % LANES, 1)
                inside = (lane >= SLOT * s) & (lane < SLOT * (s + 1))
                total = jnp.where(inside, edge, total)
            packed[f, g] = total

    def row_copy(i, f, c):
        dx, _, ring, mine = row_steps[1 + i]
        src, dst = ((head_in, h_land), (cond_in, k_land))[f]
        return pltpu.make_async_remote_copy(
            src_ref=src.at[pl.ds(CHUNK * c, CHUNK), mine],
            dst_ref=dst.at[pl.ds(CHUNK * c, CHUNK), ring],
            send_sem=row_send.at[2 * i + f, c],
            recv_sem=row_recv.at[2 * i + f, c],
            device_id=(gx + dx, gy),
            device_id_type=MESH,
        )

    def each_row(cond_of, c, act):
        for i in range(2):
            def body(i=i):
                for f in (1, 0):
                    act(row_copy(i, f, c))
            pl.when(cond_of[i])(body)
    sends_row, gets_row = (has_below, has_above), (has_above, has_below)

    def start_rows(c, _):
        each_row(sends_row, c, lambda copy: copy.start())
        return 0

    def finish_rows(c, _):
        each_row(sends_row, c, lambda copy: copy.wait_send())
        return 0

    pack_copies = []
    n = 0
    for dx, exists, ring, mine in row_steps:
        source_row = None if dx == 0 else (has_above if dx == 1 else has_below)
        for dy, side, target, source in ((1, land_l, has_right, has_left), (-1, land_r, has_left, has_right)):
            pack_copies.append((both(exists, target), both(source_row, source), pltpu.make_async_remote_copy(
                src_ref=packed.at[:, :, mine],
                dst_ref=side.at[:, :, ring],
                send_sem=pack_send.at[n],
                recv_sem=pack_recv.at[n],
                device_id=(gx + dx, gy + dy),
                device_id_type=MESH,
            )))
            n += 1
    near_rows = 1 + has_below.astype(jnp.int32) + has_above.astype(jnp.int32)
    pl.semaphore_wait(barrier, cols_n * near_rows - 1)
    for exists, _, copy in pack_copies:
        when(exists, copy.start)
    lax.fori_loop(0, chunks, start_rows, 0)

    for copy in local[2:]:
        copy.wait()
    e0 = diff[0]
    inv = 1.0 / (1.0 + e0)
    r0, f0 = e0 * inv, (moist[0] + rain[...]) * inv
    ratio[0] = r0
    moist[0] = f0

    def eliminate(layer, carry):
        upper, r, f = carry
        lower = diff[layer]
        inv = 1.0 / (1.0 + lower + upper - upper * r)
        r, f = lower * inv, (moist[layer] + upper * f) * inv
        ratio[layer] = r
        moist[layer] = f
        return lower, r, f
    lower, _, bottom = lax.fori_loop(1, depth, eliminate, (e0, r0, f0), unroll=True)
    drain = lower * bottom
    hot = one_hot_rows(tile_ref[...], offset_ref[...], count_ref[0], cols_n, tile_rows)
    mine = jnp.dot(hot, drain, precision=lax.Precision.HIGHEST, preferred_element_type=jnp.float32)
    recharge[0, gy] = mine.reshape(cols_n, tile_rows, LANES)

    rech_copies = []
    n = 0
    for i, (dx, exists, _, rows) in enumerate(row_steps):
        source_row = None if dx == 0 else (has_above if dx == 1 else has_below)
        for dy in range(0 if dx else 1, cols_n):
            to = lax.rem(gy + dy, cols_n)
            came = lax.rem(gy + cols_n - dy, cols_n)
            def copy(slot, to=to, dx=dx, i=i, rows=rows, n=n):
                return pltpu.make_async_remote_copy(
                    src_ref=recharge.at[0, gy, :, rows],
                    dst_ref=recharge.at[i, slot, :, rows],
                    send_sem=rech_send.at[n],
                    recv_sem=rech_recv.at[n],
                    device_id=(gx + dx, to),
                    device_id_type=MESH,
                )
            rech_copies.append((exists, source_row, copy(gy), copy(came)))
            n += 1
    for exists, _, out, _ in rech_copies:
        when(exists, out.start)

    def substitute(i, wet):
        layer = depth - 2 - i
        wet = moist[layer] + ratio[layer] * wet
        moist[layer] = wet
        return wet
    lax.fori_loop(0, depth - 1, substitute, bottom, unroll=True)
    wet_copy = pltpu.make_async_copy(moist, wet_out, out_sem.at[0])
    wet_copy.start()

    slabs = ring_rows // 8
    place = lax.broadcasted_iota(jnp.int32, (ring_rows, ring_cols), 0)
    ring_row = slabs * (place % 8) + place // 8
    ring_col = lax.broadcasted_iota(jnp.int32, (ring_rows, ring_cols), 1)
    row_ok = (ring_row < tile_rows) | ((ring_row < tile_rows + HALO) & has_below) | ((ring_row >= tile_rows + HALO) & has_above)
    col_ok = (ring_col < LANES) | ((ring_col < LANES + LANES // 2) & has_right) | ((ring_col >= LANES + LANES // 2) & has_left)
    mask = (row_ok & col_ok).astype(jnp.float32)
    on_grid = mask > 0.0

    for _, source, copy in pack_copies:
        when(source, copy.wait_recv)

    def interleaved(ref, *at):
        return jnp.concatenate([ref[(*at, pl.ds(i, 8, stride=slabs))] for i in range(slabs)], axis=0)

    side_on_grid = on_grid[:, LANES:]
    for g in range(groups):
        for f, dst in enumerate((h, k)):
            comb = jnp.where((lane % SLOT) < HALO, interleaved(land_l, f, g), interleaved(land_r, f, g))
            for s in range(min(per, nz - g * per)):
                side = pltpu.roll(comb, (LANES - HALO - SLOT * s) % LANES, 1)
                dst[PAD + g * per + s, :, LANES:] = jnp.where(side_on_grid, side, 0.0)

    scale = 0.5 * flow_rate
    masked = scale * mask

    def east(x):
        return pltpu.roll(x, ring_cols - 1, 1)

    def west(x):
        return pltpu.roll(x, 1, 1)

    def south(x):
        return jnp.concatenate([x[8:], pltpu.roll(x[:8], 7, 0)], axis=0)

    def north(x):
        return jnp.concatenate([pltpu.roll(x[-8:], 1, 0), x[:-8]], axis=0)

    def weights(z0):
        here = k[PAD + z0]
        up = jnp.where((z0 > 0) & (z0 < nz), scale, 0.0) * (k[PAD + z0 - 1] + here)
        for j in range(CHUNK):
            z = z0 + j
            at = PAD + z
            after = k[at + 1]
            down = jnp.where((z >= 0) & (z < nz - 1), scale, 0.0) * (here + after)
            parts = [masked * (here + turn(here)) for turn in (east, west, south, north)]
            for ref, part in zip((w_e, w_w, w_s, w_n), parts):
                ref[at] = part
            w_v[at + 1] = down
            w_d[at] = 1.0 - ((parts[0] + parts[1]) + (parts[2] + parts[3]) + (up + down))
            here, up = after, down

    def step(src, at, w_at, count):
        before, here = src[at - 1], src[at]
        out = []
        for j in range(count):
            w = w_at + j
            after = src[at + j + 1]
            out.append(
                (w_d[w] * here + w_e[w] * east(here))
                + (w_w[w] * west(here) + w_s[w] * south(here))
                + (w_n[w] * north(here) + (w_v[w] * before + w_v[w + 1] * after))
            )
            before, here = here, after
        return out

    tile_part = tile_rows // slabs

    def put_tile(at, new, add):
        for i in range(slabs):
            rows = pl.ds(i, tile_part, stride=slabs)
            part = new[8 * i : 8 * i + tile_part, 0:LANES]
            field[at, rows] = field[at, rows] + part if add else part

    def sweep(n, z0):
        src, dst = (h, h2) if n % 2 == 0 else (h2, h)
        for j, new in enumerate(step(src, PAD + z0, PAD + z0, CHUNK)):
            if n < SWEEPS - 1:
                dst[PAD + z0 + j] = new
            else:
                put_tile(PAD + z0 + j, new, False)

    surf_copies = []
    for dy in range(1, cols_n):
        to = lax.rem(gy + dy, cols_n)
        came = lax.rem(gy + cols_n - dy, cols_n)
        pair = [
            pltpu.make_async_remote_copy(
                src_ref=surf.at[gy],
                dst_ref=surf.at[slot],
                send_sem=surf_send.at[dy - 1],
                recv_sem=surf_recv.at[dy - 1],
                device_id=(gx, to),
                device_id_type=MESH,
            )
            for slot in (gy, came)
        ]
        surf_copies.append(pair)

    def finish_top():
        for _, source, _, arrived in rech_copies:
            when(source, arrived.wait_recv)

        def tile_sum(tile):
            parts = []
            for i, rows in ((0, whole), (1, last), (2, first)):
                total = recharge[i, 0, tile, rows]
                for s in range(1, cols_n):
                    total = total + recharge[i, s, tile, rows]
                parts.append(total)
            return jnp.concatenate([parts[0], parts[2], parts[1]], axis=0)
        centre = tile_sum(gy)
        right = tile_sum(jnp.minimum(gy + 1, cols_n - 1))
        left = tile_sum(jnp.maximum(gy - 1, 0))
        side = jnp.where(lane < LANES // 2, right, left)
        for z in range(SWEEPS + 3):
            delta[z] = empty
            delta2[z] = empty
        spread[0] = centre
        spread[1] = side
        start = jnp.concatenate([interleaved(spread, 0), interleaved(spread, 1)], axis=1)
        delta[1] = jnp.where(on_grid, start, 0.0)
        for n in range(SWEEPS):
            src, dst = (delta, delta2) if n % 2 == 0 else (delta2, delta)
            for z, new in enumerate(step(src, 1, PAD, min(n + 2, nz))):
                if n < SWEEPS - 1:
                    dst[z + 1] = new
                else:
                    put_tile(PAD + z, new, True)
        surf[gy] = field[PAD]
        for out, _ in surf_copies:
            out.start()

    def field_copy(c):
        return pltpu.make_async_copy(
            field.at[pl.ds(PAD + CHUNK * c, CHUNK)], field_out.at[pl.ds(CHUNK * c, CHUNK)], field_sem.at[c]
        )

    def wave(c, _):
        @pl.when(c < chunks)
        def _():
            each_row(gets_row, c, lambda copy: copy.wait_recv())
            for j in range(CHUNK):
                z = CHUNK * c + j
                for src, dst in ((h_land, h), (k_land, k)):
                    dst[PAD + z, :, 0:LANES] = interleaved(src, z)

        weights(CHUNK * c - 1)
        for n in range(SWEEPS):
            sweep(n, CHUNK * c - (n + 1))
        pl.when(c == 1)(finish_top)
        pl.when(c >= 2)(lambda: field_copy(c - 2).start())
        return 0
    lax.fori_loop(0, chunks + 1, wave, 0)

    field_copy(chunks - 1).start()
    for _, arrived in surf_copies:
        arrived.wait_recv()
    surf_copy = pltpu.make_async_copy(surf, surf_out, out_sem.at[2])
    surf_copy.start()

    lax.fori_loop(0, chunks, finish_rows, 0)
    for exists, _, copy in pack_copies:
        when(exists, copy.wait_send)
    for exists, _, out, _ in rech_copies:
        when(exists, out.wait_send)
    for out, _ in surf_copies:
        out.wait_send()
    wet_copy.wait()
    for c in range(chunks):
        field_copy(c).wait()
    surf_copy.wait()


def exchange_kernel(
    tile_rows, cols_n,
    field_in, wet_in, surf_in, tile_in, offset_in, patch_in, count_ref,
    head_out, moist_out, patch_out,
    field, wet, surf, tile_ref, offset_ref, patch_ref, sem,
):
    depth, blocks, _ = wet.shape
    upper = pl.ds(0, depth - 1)
    loads = [
        pltpu.make_async_copy(src, dst, sem.at[i])
        for i, (src, dst) in enumerate((
            (tile_in, tile_ref),
            (offset_in, offset_ref),
            (patch_in, patch_ref),
            (surf_in, surf),
            (wet_in.at[depth - 1], wet.at[depth - 1]),
            (wet_in.at[upper], wet.at[upper]),
            (field_in, field),
        ))
    ]
    for copy in loads:
        copy.start()
    for copy in loads[:5]:
        copy.wait()
    hot = one_hot_rows(tile_ref[...], offset_ref[...], count_ref[0], cols_n, tile_rows)
    surface = surf[...].reshape(cols_n * tile_rows, LANES)
    saturation = lax.dot_general(
        hot, surface, (((0,), (0,)), ((), ())),
        precision=lax.Precision.HIGHEST, preferred_element_type=jnp.float32,
    )
    patch = lax.broadcasted_iota(jnp.int32, (PATCH_DEV, blocks), 0)
    patch_hot = (patch == patch_ref[...]).astype(jnp.float32)
    patch_out[...] = jnp.dot(
        patch_hot, saturation, precision=lax.Precision.HIGHEST, preferred_element_type=jnp.float32
    )
    used = (lax.broadcasted_iota(jnp.int32, (blocks, LANES), 0) < count_ref[0]).astype(jnp.float32)
    wet_bottom = wet[depth - 1]
    wet[depth - 1] = wet_bottom + capillary * (saturation - used * wet_bottom)
    stores = [
        pltpu.make_async_copy(wet.at[depth - 1], moist_out.at[depth - 1], sem.at[0]),
        pltpu.make_async_copy(wet.at[upper], moist_out.at[upper], sem.at[1]),
        pltpu.make_async_copy(field, head_out, sem.at[2]),
    ]
    stores[0].start()
    for load, store in zip(loads[5:], stores[1:]):
        load.wait()
        store.start()
    for store in stores:
        store.wait()


def local(rows_n, cols_n, moisture, diffusivity, rain, head, conductivity, tile_ids, offsets, patch_ids, counts):
    blocks, depth, _ = moisture.shape
    nz, tile_rows, _ = head.shape
    moisture = jnp.transpose(moisture, (1, 0, 2))
    diffusivity = jnp.transpose(diffusivity, (1, 0, 2))
    tile_ids, offsets, patch_ids = (x.reshape(1, blocks) for x in (tile_ids, offsets, patch_ids))
    f32 = jnp.float32
    per = LANES // SLOT
    groups = pl.cdiv(nz, per)
    ring = (tile_rows + 2 * HALO, 2 * LANES)
    hbm = pl.BlockSpec(memory_space=pltpu.HBM)
    vmem = pl.BlockSpec(memory_space=pltpu.VMEM)
    smem = pl.BlockSpec(memory_space=pltpu.SMEM)
    dma = pltpu.SemaphoreType.DMA
    rech = 3 * cols_n - 1
    field, wet, surf = pl.pallas_call(
        functools.partial(flow_kernel, (rows_n, cols_n, nz, tile_rows)),
        name="flow",
        out_shape=(
            jax.ShapeDtypeStruct((nz, tile_rows, LANES), f32),
            jax.ShapeDtypeStruct((depth, blocks, LANES), f32),
            jax.ShapeDtypeStruct((cols_n, tile_rows, LANES), f32),
        ),
        in_specs=[hbm] * 7 + [smem],
        out_specs=(hbm,) * 3,
        scratch_shapes=[
            pltpu.VMEM((nz, ring[0], LANES), f32),
            pltpu.VMEM((nz, ring[0], LANES), f32),
            pltpu.VMEM((2, ring[0], LANES), f32),
            pltpu.VMEM((nz + 2 * PAD,) + ring, f32),
            pltpu.VMEM((nz + 2 * PAD,) + ring, f32),
            pltpu.VMEM((nz + 2 * PAD,) + ring, f32),
            pltpu.VMEM((nz + 2 * PAD, tile_rows, LANES), f32),
            pltpu.VMEM((nz + 2 * PAD,) + ring, f32),
            pltpu.VMEM((nz + 2 * PAD,) + ring, f32),
            pltpu.VMEM((nz + 2 * PAD,) + ring, f32),
            pltpu.VMEM((nz + 2 * PAD,) + ring, f32),
            pltpu.VMEM((nz + 2 * PAD,) + ring, f32),
            pltpu.VMEM((nz + 2 * PAD,) + ring, f32),
            pltpu.VMEM((SWEEPS + 3,) + ring, f32),
            pltpu.VMEM((SWEEPS + 3,) + ring, f32),
            pltpu.VMEM((2, groups, tile_rows, LANES), f32),
            pltpu.VMEM((2, groups, ring[0], LANES), f32),
            pltpu.VMEM((2, groups, ring[0], LANES), f32),
            pltpu.VMEM((depth, blocks, LANES), f32),
            pltpu.VMEM((depth, blocks, LANES), f32),
            pltpu.VMEM((depth, blocks, LANES), f32),
            pltpu.VMEM((blocks, LANES), f32),
            pltpu.VMEM((1, blocks), jnp.int32),
            pltpu.VMEM((1, blocks), jnp.int32),
            pltpu.VMEM((3, cols_n, cols_n, tile_rows, LANES), f32),
            pltpu.VMEM((cols_n, tile_rows, LANES), f32),
            dma((7,)), dma((3,)), dma((nz // CHUNK,)), dma((4, nz // CHUNK)), dma((4, nz // CHUNK)), dma((6,)), dma((6,)),
            dma((rech,)), dma((rech,)), dma((cols_n,)), dma((cols_n,)),
        ],
        compiler_params=pltpu.CompilerParams(
            collective_id=0, has_side_effects=True, vmem_limit_bytes=63 * 1024 * 1024
        ),
    )(moisture, diffusivity, rain, head, conductivity, tile_ids, offsets, counts)
    head_out, moist_out, patch_sums = pl.pallas_call(
        functools.partial(exchange_kernel, tile_rows, cols_n),
        name="exchange",
        out_shape=(
            jax.ShapeDtypeStruct((nz, tile_rows, LANES), f32),
            jax.ShapeDtypeStruct((depth, blocks, LANES), f32),
            jax.ShapeDtypeStruct((PATCH_DEV, LANES), f32),
        ),
        in_specs=[hbm] * 6 + [smem],
        out_specs=(hbm, hbm, vmem),
        scratch_shapes=[
            pltpu.VMEM((nz, tile_rows, LANES), f32),
            pltpu.VMEM((depth, blocks, LANES), f32),
            pltpu.VMEM((cols_n, tile_rows, LANES), f32),
            pltpu.VMEM((1, blocks), jnp.int32),
            pltpu.VMEM((1, blocks), jnp.int32),
            pltpu.VMEM((1, blocks), jnp.int32),
            dma((7,)),
        ],
        compiler_params=pltpu.CompilerParams(vmem_limit_bytes=63 * 1024 * 1024),
    )(field, wet, surf, tile_ids, offsets, patch_ids, counts)
    return head_out, jnp.transpose(moist_out, (1, 0, 2)), patch_sums


def solution(mesh):
    placed = (
        P(("gx", "gy"), None, None),
        P(("gx", "gy"), None, None),
        P(("gx", "gy"), None),
        P(None, "gx", "gy"),
        P(None, "gx", "gy"),
        P(("gx", "gy")),
        P(("gx", "gy")),
        P(("gx", "gy")),
        P(("gx", "gy")),
    )
    return jax.shard_map(
        functools.partial(local, mesh.shape["gx"], mesh.shape["gy"]),
        mesh=mesh,
        in_specs=placed,
        out_specs=(P(None, "gx", "gy"), P(("gx", "gy"), None, None), P(("gx", "gy"), None)),
        check_vma=False,
    )
```
